256 devices in a mesh: frames: 16 (over z, core), heads: 4 (over x), dp: 4 (over y).
Axes of the slice: x: 4, y: 4, z: 8, core: 2. Of those that a mesh axis runs over, the one named last changes fastest.
Arguments:
- queries: bfloat16 [10240, 4096], P(('dp', 'frames'), 'heads'), parts along dimension 0, may hold values from -10 to 10
- key_vectors: bfloat16 [10240, 4096], P(('dp', 'frames'), 'heads'), parts along dimension 0, may hold values from -4 to 4
- values: bfloat16 [10240, 4096], P(('dp', 'frames'), 'heads'), parts along dimension 0, may hold values from -5 to 5
- grad_output: bfloat16 [10240, 4096], P(('dp', 'frames'), 'heads'), parts along dimension 0, may hold values from -5 to 5
- segment_index: int32 [10240], P(('dp', 'frames')), parts along dimension 0, may hold values from 0 to 63, as said below
Outputs:
- attended: bfloat16 [10240, 4096], P(('dp', 'frames'), 'heads'), parts along dimension 0
- grad_queries: bfloat16 [10240, 4096], P(('dp', 'frames'), 'heads'), parts along dimension 0
- grad_keys: bfloat16 [10240, 4096], P(('dp', 'frames'), 'heads'), parts along dimension 0
- grad_values: bfloat16 [10240, 4096], P(('dp', 'frames'), 'heads'), parts along dimension 0
The draws below stay inside these ranges and needn't reach their ends.
There are 4 independent parts, one for each index of `dp`. The reference program is written for one: setup_inputs(seed, part) draws one part's arguments, and reference() takes and returns one part's arrays. A program takes and returns all parts, laid end to end along the dimension named above; each array names one. Nothing has to cross between parts.
Inputs may be any that keep to these rules, and one draw needn't show every extreme that they name: `segment_index`: rows are stored in paired order: the first 80 rows of frames index g are the natural positions g * 80 onward, its last 80 rows the positions (31 - g) * 80 onward. Along natural positions the segment never falls, starts at 0 (the reference-image prefix), and each of the 64 segments holds at least one position.
All inputs are finite; a program needn't handle non-finite values.
Results may differ from the reference program's by a relative error of at most 0.014.
Values may be sent and summed in bfloat16 or wider, within the bound.
A program may use at most 128 MiB of HBM per device.

```python
import math
import jax
import jax.numpy as jnp
from jax import lax

HEADS = 32
HEAD_DIM = 128
TOK_DEV = 160
TOKENS = 2560
GROUPS = 64
BLOCKS = 32
HALF = 80


def drawn_pair(key):
    shape = (TOKENS, HEADS * HEAD_DIM)
    query_rows = jax.random.truncated_normal(jax.random.fold_in(key, 36), -4.0, 4.0, shape)
    key_rows = jax.random.truncated_normal(jax.random.fold_in(key, 37), -4.0, 4.0, shape)
    return (query_rows.astype(jnp.float32), key_rows.astype(jnp.float32))


def draw_queries(key, part):
    return drawn_pair(key)[0].astype(jnp.bfloat16)


def draw_key_vectors(key, part):
    return drawn_pair(key)[1].astype(jnp.bfloat16)


def draw_segment_index(key, part):
    cuts = jax.random.permutation(jax.random.fold_in(key, 21), TOKENS - 1)[:GROUPS - 1] + 1
    positions = jnp.arange(TOKENS)
    natural = jnp.sum((cuts[None, :] <= positions[:, None]).astype(jnp.int32), axis=1).astype(jnp.int32)
    owner = positions // TOK_DEV
    inside = positions % TOK_DEV
    half_block = jnp.where(inside // HALF == 0, owner, BLOCKS - 1 - owner)
    natural_pos = (half_block * HALF + inside % HALF).astype(jnp.int32)
    return natural[natural_pos].astype(jnp.int32)


def steps_of(key, dims, split, low, top_value):
    def one(axis_at, parts):
        draws = jax.random.uniform(jax.random.fold_in(jax.random.fold_in(key, 6), axis_at), (parts,), jnp.float32, low / len(split), top_value / len(split))
        return jnp.repeat(jnp.exp(draws), dims[axis_at] // parts).reshape((-1,) + (1,) * (len(dims) - axis_at - 1))

    factor_of = one(*split[0])
    for cut in split[1:]:
        factor_of = factor_of * one(*cut)
    return factor_of


def scatter_about(own_key, extent, width, most, pieces=(), held_as=jnp.bfloat16):
    values = width * jax.random.normal(own_key, extent, jnp.float32)
    if pieces:
        values = values * steps_of(own_key, extent, pieces, -0.22, 0.18)
    return jnp.clip(values, -most, most).astype(held_as)


def setup_inputs(seed: int = 0, part: int = 0) -> dict:
    streams_of = jax.random.split(jax.random.key(seed), 6)
    own_keys = jax.random.split(jax.random.fold_in(streams_of[5], part), 6)
    queries = draw_queries(jax.random.fold_in(jax.random.fold_in(streams_of[5], part), 71), part)
    key_vectors = draw_key_vectors(jax.random.fold_in(jax.random.fold_in(streams_of[5], part), 71), part)
    values = scatter_about(own_keys[2], (TOKENS, HEADS * HEAD_DIM), 1.0, 5.0, ((0, 16), (1, 4)))
    grad_output = scatter_about(own_keys[3], (TOKENS, HEADS * HEAD_DIM), 1.0, 5.0, ((0, 16), (1, 4)))
    segment_index = draw_segment_index(jax.random.fold_in(jax.random.fold_in(streams_of[5], part), 71), part)
    return dict(queries=queries, key_vectors=key_vectors, values=values, grad_output=grad_output, segment_index=segment_index)


def reference(queries, key_vectors, values, grad_output, segment_index):
    scale_factor = 1.0 / math.sqrt(HEAD_DIM)
    seen_mask = segment_index[None, :] <= segment_index[:, None]

    def split_heads(array):
        return array.reshape(TOKENS, HEADS, HEAD_DIM).transpose(1, 0, 2)

    def merge_heads(array):
        return array.transpose(1, 0, 2).reshape(TOKENS, HEADS * HEAD_DIM)

    def one_head(items):
        query_head, key_head, value_head, grad_head = items
        scores = jnp.dot(query_head, key_head.T, preferred_element_type=jnp.float32) * scale_factor
        row_max = lax.optimization_barrier(jnp.max(jnp.where(seen_mask, scores, -jnp.inf), axis=1, keepdims=True))
        exp_sum = lax.optimization_barrier(jnp.sum(jnp.where(seen_mask, jnp.exp(scores - row_max), 0.0), axis=1, keepdims=True))
        log_total = row_max + jnp.log(exp_sum)
        soft_weights = jnp.where(seen_mask, jnp.exp(scores - log_total), 0.0)
        weights_low = soft_weights.astype(jnp.bfloat16)
        attended = jnp.dot(weights_low, value_head, preferred_element_type=jnp.float32).astype(jnp.bfloat16)
        row_delta = lax.optimization_barrier(jnp.sum(grad_head.astype(jnp.float32) * attended.astype(jnp.float32), axis=1, keepdims=True))
        grad_weights = jnp.dot(grad_head, value_head.T, preferred_element_type=jnp.float32)
        grad_scores = (soft_weights * (grad_weights - row_delta)).astype(jnp.bfloat16)
        grad_query = (jnp.dot(grad_scores, key_head, preferred_element_type=jnp.float32) * scale_factor).astype(jnp.bfloat16)
        grad_key = (jnp.dot(grad_scores.T, query_head, preferred_element_type=jnp.float32) * scale_factor).astype(jnp.bfloat16)
        grad_value = jnp.dot(weights_low.T, grad_head, preferred_element_type=jnp.float32).astype(jnp.bfloat16)
        return (attended, grad_query, grad_key, grad_value)
    results = lax.map(one_head, (split_heads(queries), split_heads(key_vectors), split_heads(values), split_heads(grad_output)))
    return (merge_heads(results[0]), merge_heads(results[1]), merge_heads(results[2]), merge_heads(results[3]))
```

```python
import functools
import math

import jax
import jax.numpy as jnp
from jax import lax
from jax.experimental import pallas as pl
from jax.experimental.pallas import tpu as pltpu
from jax.sharding import PartitionSpec as P

HEAD_DIM = 128
MESH = pl.DeviceIdType.MESH
ROWS = 160
CHIPS = 8
OWN = CHIPS * ROWS
ALL = 2 * OWN
RB = 256
KC = 512
HIDDEN = -float(2**30)
SCALE = 1.0 / math.sqrt(HEAD_DIM)
SCALE2 = SCALE * math.log2(math.e)
ORDER = (4, 3, 5, 2, 6, 1, 7)
F32, BF16 = jnp.float32, jnp.bfloat16


def dot_rows(a, b):
    return lax.dot_general(a, b, (((1,), (1,)), ((), ())), preferred_element_type=F32)


def dot_plain(a, b):
    return lax.dot_general(a, b, (((1,), (0,)), ((), ())), preferred_element_type=F32)


def kernel(
    q_ref, k_ref, v_ref, g_ref, seg_ref,
    o_out, dq_out, dk_out, dv_out,
    qb, kb, vb, gb, segown, segb, eb, ab, db, vt, kt, sb, pb, inv, obuf, gn, qn,
    keep, give, got, dqb, dkb, dvb,
    in_send, in_recv, loc, fw_send, fw_recv, out_send, out_recv, out_loc, x_send, x_recv,
):
    me = lax.axis_index("frames")
    z, c = me // 2, lax.rem(me, 2)
    other = z * 2 + 1 - c

    def peer(d):
        return lax.rem(z + d, CHIPS)

    def cols(i):
        return pl.ds(pl.multiple_of(i * HEAD_DIM, HEAD_DIM), HEAD_DIM)

    def rows(i):
        return pl.ds(pl.multiple_of(i * ROWS, ROWS), ROWS)

    def krows(core, i):
        return pl.ds(pl.multiple_of((core * CHIPS + i) * ROWS, ROWS), ROWS)

    segown[:, :ROWS] = jnp.broadcast_to(seg_ref[...].astype(F32), (8, ROWS))
    segown[:, ROWS:] = jnp.zeros((8, 2 * HEAD_DIM - ROWS), F32)

    barrier = pltpu.get_barrier_semaphore()
    for d in ORDER:
        pl.semaphore_signal(barrier, inc=1, device_id={"frames": peer(d) * 2 + c}, device_id_type=MESH)
    pl.semaphore_signal(barrier, inc=1, device_id={"frames": other}, device_id_type=MESH)
    pl.semaphore_wait(barrier, CHIPS)

    def parts(a, head, source):
        if a == 4:
            return segown, segb.at[c, source]
        ref, buf = ((k_ref, kb), (q_ref, qb), (v_ref, vb), (g_ref, gb))[a]
        where = krows(c, source) if a in (0, 2) else rows(source)
        return ref.at[:, cols(head)], buf.at[where]

    def in_copy(a, d):
        src, dst = parts(a, peer(d), z)
        return pltpu.make_async_remote_copy(
            src, dst, in_send.at[a, d], in_recv.at[a, d],
            device_id={"frames": peer(d) * 2 + c}, device_id_type=MESH)

    def in_arrival(a, d):
        src, dst = parts(a, z, lax.rem(z + CHIPS - d, CHIPS))
        return pltpu.make_async_remote_copy(
            src, dst, in_send.at[a, d], in_recv.at[a, d],
            device_id={"frames": peer(d) * 2 + c}, device_id_type=MESH)

    def own_copy(a):
        src, dst = parts(a, z, z)
        return pltpu.make_async_copy(src, dst, loc.at[a])

    for a in (4, 0, 1, 2, 3):
        own_copy(a).start()
        for d in ORDER:
            in_copy(a, d).start()

    def landed(a):
        own_copy(a).wait()
        for d in ORDER:
            in_arrival(a, d).wait_recv()

    def forward(a, d):
        buf = kb if a == 0 else vb
        where = krows(c, lax.rem(z + CHIPS - d, CHIPS))
        return pltpu.make_async_remote_copy(
            buf.at[where], buf.at[where], fw_send.at[a, d], fw_recv.at[a, d],
            device_id={"frames": other}, device_id_type=MESH)

    def forwarded(a, d):
        buf = kb if a == 0 else vb
        where = krows(1 - c, lax.rem(z + CHIPS - d, CHIPS))
        return pltpu.make_async_remote_copy(
            buf.at[where], buf.at[where], fw_send.at[a, d], fw_recv.at[a, d],
            device_id={"frames": other}, device_id_type=MESH)

    def share(a):
        own_copy(a).wait()
        forward(a, 0).start()
        for d in (1, 7, 2, 6, 3, 5, 4):
            in_arrival(a, d).wait_recv()
            forward(a, d).start()

    landed(4)
    seg_fw = pltpu.make_async_remote_copy(
        segb.at[c], segb.at[c], fw_send.at[1, 0], fw_recv.at[1, 0],
        device_id={"frames": other}, device_id_type=MESH)
    seg_fw.start()
    lane = lax.broadcasted_iota(jnp.int32, (ROWS, HEAD_DIM), 1).astype(F32)

    def segment_rows(core, i):
        row = segb[core, i][0:1, :]
        return jnp.transpose(jnp.broadcast_to(row, (HEAD_DIM, 2 * HEAD_DIM)))[:ROWS]

    def own_rows(i, _):
        seg = segment_rows(c, i)
        eb[krows(c, i), :] = jnp.where(seg == lane, 1.0, 0.0).astype(BF16)
        ab[rows(i), :] = jnp.where(lane > seg, HIDDEN, 0.0).astype(BF16)
        return 0

    lax.fori_loop(0, CHIPS, own_rows, 0)
    seg_fw.wait_send()
    pltpu.make_async_remote_copy(
        segb.at[1 - c], segb.at[1 - c], fw_send.at[1, 0], fw_recv.at[1, 0],
        device_id={"frames": other}, device_id_type=MESH).wait_recv()

    def other_rows(i, _):
        eb[krows(1 - c, i), :] = jnp.where(segment_rows(1 - c, i) == lane, 1.0, 0.0).astype(BF16)
        return 0

    lax.fori_loop(0, CHIPS, other_rows, 0)

    share(0)
    landed(1)
    for d in range(CHIPS):
        forwarded(0, d).wait_recv()
    for i in range(ALL // KC):
        kt[:, i * KC : (i + 1) * KC] = jnp.transpose(kb[i * KC : (i + 1) * KC, :].astype(F32)).astype(BF16)

    def block(i):
        return pl.ds(pl.multiple_of(i * RB, RB), RB)

    def weights_step(i, _):
        qx = jnp.concatenate([qb[block(i), :], ab[block(i), :]], axis=1)
        most = jnp.full((8, RB), -jnp.inf, F32)
        for j in range(ALL // KC):
            at = slice(j * KC, (j + 1) * KC)
            kx = jnp.concatenate([kb[at, :], eb[at, :]], axis=1)
            s = dot_rows(kx, qx)
            sb[at, :] = s
            most = jnp.maximum(most, jnp.max(s.reshape(KC // 8, 8, RB), axis=0))
        top = jnp.max(most, axis=0, keepdims=True) * SCALE2
        for j in range(ALL // KC):
            at = slice(j * KC, (j + 1) * KC)
            pb[i, at, :] = jnp.exp2(sb[at, :] * SCALE2 - top).astype(BF16)
        return 0

    lax.fori_loop(0, OWN // RB, weights_step, 0)

    share(2)
    for d in range(CHIPS):
        forwarded(2, d).wait_recv()
    vt[HEAD_DIM:, :] = jnp.ones((HEAD_DIM, ALL), BF16)
    for i in range(ALL // KC):
        vt[:HEAD_DIM, i * KC : (i + 1) * KC] = jnp.transpose(vb[i * KC : (i + 1) * KC, :].astype(F32)).astype(BF16)

    def output_step(i, _):
        both = jnp.transpose(dot_plain(vt[...], pb[i]))
        part = 1.0 / both[:, HEAD_DIM:]
        inv[block(i), :] = part
        obuf[block(i), :] = (both[:, :HEAD_DIM] * part).astype(BF16)
        return 0

    lax.fori_loop(0, OWN // RB, output_step, 0)

    outs = ((obuf, o_out), (dvb, dv_out), (dqb, dq_out), (dkb, dk_out))

    def out_copy(a, d):
        buf, out = outs[a]
        return pltpu.make_async_remote_copy(
            buf.at[rows(peer(d))], out.at[:, cols(z)], out_send.at[a, d], out_recv.at[a, d],
            device_id={"frames": peer(d) * 2 + c}, device_id_type=MESH)

    def out_arrival(a, d):
        buf, out = outs[a]
        source = lax.rem(z + CHIPS - d, CHIPS)
        return pltpu.make_async_remote_copy(
            buf.at[rows(source)], out.at[:, cols(source)], out_send.at[a, d], out_recv.at[a, d],
            device_id={"frames": peer(d) * 2 + c}, device_id_type=MESH)

    def out_own(a):
        buf, out = outs[a]
        return pltpu.make_async_copy(buf.at[rows(z)], out.at[:, cols(z)], out_loc.at[a])

    def send_back(a):
        for d in ORDER:
            out_copy(a, d).start()
        out_own(a).start()

    send_back(0)

    landed(3)
    narrow = lax.broadcasted_iota(jnp.int32, (RB, HEAD_DIM), 1)

    def delta_step(i, _):
        g = gb[block(i), :].astype(F32)
        part = inv[block(i), :]
        gn[block(i), :] = (g * part).astype(BF16)
        qn[block(i), :] = (qb[block(i), :].astype(F32) * (part * SCALE)).astype(BF16)
        delta = -jnp.sum(g * obuf[block(i), :].astype(F32), axis=1, keepdims=True)
        first = delta.astype(BF16).astype(F32)
        second = (delta - first).astype(BF16).astype(F32)
        third = delta - first - second
        cells = jnp.where(narrow == 0, first, jnp.where(narrow == 1, second, jnp.where(narrow == 2, third, 0.0)))
        db[block(i), :] = cells.astype(BF16)
        return 0

    lax.fori_loop(0, OWN // RB, delta_step, 0)

    def key_sums(right, a, result):
        def terms(core, j):
            at = pl.ds(pl.multiple_of(core * OWN + j * RB, RB), RB)
            total = dot_plain(pb[0, at, :], right[0:RB, :])
            for i in range(1, OWN // RB):
                total = total + dot_plain(pb[i, at, :], right[i * RB : (i + 1) * RB, :])
            return total

        def swap(j):
            at = slice(j * RB, (j + 1) * RB)
            return pltpu.make_async_remote_copy(
                give.at[a, at], got.at[a, at], x_send.at[a, j], x_recv.at[a, j],
                device_id={"frames": other}, device_id_type=MESH)

        for j in range(OWN // RB):
            give[a, j * RB : (j + 1) * RB, :] = terms(1 - c, j)
            swap(j).start()

        def mine(j, _):
            keep[block(j), :] = terms(c, j)
            return 0

        lax.fori_loop(0, OWN // RB, mine, 0)
        for j in range(OWN // RB):
            at = slice(j * RB, (j + 1) * RB)
            swap(j).wait()
            result[at, :] = (keep[at, :] + got[a, at, :]).astype(BF16)

    key_sums(gn, 0, dvb)
    send_back(1)

    ones = jnp.ones((KC, HEAD_DIM), BF16)

    def grad_step(i, _):
        gx = jnp.concatenate([gb[block(i), :], db[block(i), :]], axis=1)
        for j in range(ALL // KC):
            at = slice(j * KC, (j + 1) * KC)
            vx = jnp.concatenate([vb[at, :], ones], axis=1)
            pb[i, at, :] = (pb[i, at, :].astype(F32) * dot_rows(vx, gx)).astype(BF16)
        dq = jnp.transpose(dot_plain(kt[...], pb[i]))
        dqb[block(i), :] = (dq * (inv[block(i), :] * SCALE)).astype(BF16)
        return 0

    lax.fori_loop(0, OWN // RB, grad_step, 0)
    send_back(2)
    key_sums(qn, 1, dkb)
    send_back(3)

    for a in range(5):
        for d in ORDER:
            in_copy(a, d).wait_send()
    for a in (0, 2):
        for d in range(CHIPS):
            forward(a, d).wait_send()
    for a in range(4):
        out_own(a).wait()
        for d in ORDER:
            out_copy(a, d).wait_send()
            out_arrival(a, d).wait_recv()


def shards(queries, key_vectors, values, grad_output, segment_index):
    vmem, sems = pltpu.VMEM, pltpu.SemaphoreType.DMA
    out = jax.ShapeDtypeStruct(queries.shape, BF16)
    any_spec = pl.BlockSpec(memory_space=pl.ANY)
    vmem_spec = pl.BlockSpec(memory_space=pltpu.VMEM)
    attended, grad_queries, grad_keys, grad_values = pl.pallas_call(
        kernel,
        out_shape=[out] * 4,
        in_specs=[any_spec] * 4 + [vmem_spec],
        out_specs=[OUT_SPEC] * 4,
        scratch_shapes=[
            vmem((OWN, HEAD_DIM), BF16),
            vmem((ALL, HEAD_DIM), BF16),
            vmem((ALL, HEAD_DIM), BF16),
            vmem((OWN, HEAD_DIM), BF16),
            vmem((8, 2 * HEAD_DIM), F32),
            vmem((2, CHIPS, 8, 2 * HEAD_DIM), F32),
            vmem((ALL, HEAD_DIM), BF16),
            vmem((OWN, HEAD_DIM), BF16),
            vmem((OWN, HEAD_DIM), BF16),
            vmem((2 * HEAD_DIM, ALL), BF16),
            vmem((HEAD_DIM, ALL), BF16),
            vmem((ALL, RB), F32),
            vmem((OWN // RB, ALL, RB), BF16),
            vmem((OWN, HEAD_DIM), F32),
            vmem((OWN, HEAD_DIM), BF16),
            vmem((OWN, HEAD_DIM), BF16),
            vmem((OWN, HEAD_DIM), BF16),
            vmem((OWN, HEAD_DIM), F32),
            vmem((2, OWN, HEAD_DIM), F32),
            vmem((2, OWN, HEAD_DIM), F32),
            vmem((OWN, HEAD_DIM), BF16),
            vmem((OWN, HEAD_DIM), BF16),
            vmem((OWN, HEAD_DIM), BF16),
            sems((5, CHIPS)),
            sems((5, CHIPS)),
            sems((5,)),
            sems((3, CHIPS)),
            sems((3, CHIPS)),
            sems((4, CHIPS)),
            sems((4, CHIPS)),
            sems((4,)),
            sems((2, OWN // RB)),
            sems((2, OWN // RB)),
        ],
        compiler_params=pltpu.CompilerParams(
            collective_id=0, has_side_effects=True, vmem_limit_bytes=56 << 20
        ),
        cost_estimate=pl.CostEstimate(
            flops=12 * OWN * ALL * HEAD_DIM, bytes_accessed=8 * ROWS * 1024 * 2, transcendentals=OWN * ALL
        ),
    )(queries, key_vectors, values, grad_output, segment_index.reshape(1, ROWS))
    return (attended, grad_queries, grad_keys, grad_values)


OUT_SPEC = pl.BlockSpec(memory_space=pl.ANY)


def solution(mesh):
    wide = P(("dp", "frames"), "heads")
    return jax.shard_map(
        shards,
        mesh=mesh,
        in_specs=(wide, wide, wide, wide, P(("dp", "frames"))),
        out_specs=(wide, wide, wide, wide),
        check_vma=False,
    )
```

```python
import functools
import math

import jax
import jax.numpy as jnp
from jax import lax
from jax.experimental import pallas as pl
from jax.experimental.pallas import tpu as pltpu
from jax.sharding import PartitionSpec as P

HEAD_DIM = 128
MESH = pl.DeviceIdType.MESH
ROWS = 160
CHIPS = 8
OWN = CHIPS * ROWS
ALL = 2 * OWN
RB = 256
KC = 512
HIDDEN = -float(2**30)
SCALE = 1.0 / math.sqrt(HEAD_DIM)
SCALE2 = SCALE * math.log2(math.e)
PIECE = RB // CHIPS
BLOCKS = OWN // RB
GROUPS = ((0, 2), (2, 5))
ORDER = ((4, 4), (3, 5), (5, 3), (2, 6), (6, 2), (1, 7), (7, 1))
F32, BF16 = jnp.float32, jnp.bfloat16


def dot_rows(a, b):
    return lax.dot_general(a, b, (((1,), (1,)), ((), ())), preferred_element_type=F32)


def dot_plain(a, b):
    return lax.dot_general(a, b, (((1,), (0,)), ((), ())), preferred_element_type=F32)


def kernel(
    q_ref, k_ref, v_ref, g_ref, seg_ref,
    o_out, dq_out, dk_out, dv_out,
    qb, kb, vb, gb, segin, segown, segb, eb, ab, vt, kt, sb, pb, ds, inv, obuf, gn, qn,
    give, got, dqb, dkb, dvb,
    seg_sem, in_send, in_recv, loc, g_send, g_recv, g_loc, fw_send, fw_recv, out_send, out_recv, out_loc, x_send, x_recv,
):
    me = lax.axis_index("frames")
    z, c = me // 2, lax.rem(me, 2)
    other = z * 2 + 1 - c

    def peer(d):
        return lax.rem(z + d, CHIPS)

    def cols(i):
        return pl.ds(pl.multiple_of(i * HEAD_DIM, HEAD_DIM), HEAD_DIM)

    def rows(i):
        return pl.ds(pl.multiple_of(i * ROWS, ROWS), ROWS)

    def krows(core, i):
        return pl.ds(pl.multiple_of((core * CHIPS + i) * ROWS, ROWS), ROWS)

    seg_copy = pltpu.make_async_copy(seg_ref, segin, seg_sem)
    seg_copy.start()

    barrier = pltpu.get_barrier_semaphore()
    for d in range(1, CHIPS):
        pl.semaphore_signal(barrier, inc=1, device_id={"frames": peer(d) * 2 + c}, device_id_type=MESH)
    pl.semaphore_signal(barrier, inc=1, device_id={"frames": other}, device_id_type=MESH)
    seg_copy.wait()
    segown[:, :ROWS] = jnp.broadcast_to(segin[...].astype(F32), (8, ROWS))
    segown[:, ROWS:] = jnp.zeros((8, 2 * HEAD_DIM - ROWS), F32)
    pl.semaphore_wait(barrier, CHIPS)

    def parts(a, head, source):
        if a == 4:
            return segown, segb.at[c, source]
        if a == 1:
            return q_ref.at[:, :, cols(head)], qb.at[:, source]
        ref, buf = (k_ref, kb) if a == 0 else (v_ref, vb)
        return ref.at[:, cols(head)], buf.at[krows(c, source)]

    def in_copy(a, d):
        src, dst = parts(a, peer(d), z)
        return pltpu.make_async_remote_copy(
            src, dst, in_send.at[a, d], in_recv.at[a, d],
            device_id={"frames": peer(d) * 2 + c}, device_id_type=MESH)

    def in_arrival(a, d):
        src, dst = parts(a, z, lax.rem(z + CHIPS - d, CHIPS))
        return pltpu.make_async_remote_copy(
            src, dst, in_send.at[a, d], in_recv.at[a, d],
            device_id={"frames": peer(d) * 2 + c}, device_id_type=MESH)

    def own_copy(a):
        src, dst = parts(a, z, z)
        return pltpu.make_async_copy(src, dst, loc.at[a])

    def g_parts(group, head, source):
        span = pl.ds(GROUPS[group][0], GROUPS[group][1] - GROUPS[group][0])
        return g_ref.at[span, :, cols(head)], gb.at[span, source]

    def g_copy(group, d, head, source):
        src, dst = g_parts(group, head, source)
        return pltpu.make_async_remote_copy(
            src, dst, g_send.at[group, d], g_recv.at[group, d],
            device_id={"frames": peer(d) * 2 + c}, device_id_type=MESH)

    def g_own(group):
        src, dst = g_parts(group, z, z)
        return pltpu.make_async_copy(src, dst, g_loc.at[group])

    turns = [a if a == b else jnp.where(c == 0, a, b) for a, b in ORDER]
    for a in (4, 0, 1, 2):
        for d in turns:
            in_copy(a, d).start()
        own_copy(a).start()
    for group in range(len(GROUPS)):
        for d in turns:
            g_copy(group, d, peer(d), z).start()
        g_own(group).start()

    def landed(a):
        own_copy(a).wait()
        for d in range(1, CHIPS):
            in_arrival(a, d).wait_recv()

    def forward(a, d):
        buf = kb if a == 0 else vb
        where = krows(c, lax.rem(z + CHIPS - d, CHIPS))
        return pltpu.make_async_remote_copy(
            buf.at[where], buf.at[where], fw_send.at[a, d], fw_recv.at[a, d],
            device_id={"frames": other}, device_id_type=MESH)

    def forwarded(a, d):
        buf = kb if a == 0 else vb
        where = krows(1 - c, lax.rem(z + CHIPS - d, CHIPS))
        return pltpu.make_async_remote_copy(
            buf.at[where], buf.at[where], fw_send.at[a, d], fw_recv.at[a, d],
            device_id={"frames": other}, device_id_type=MESH)

    def share(a):
        own_copy(a).wait()
        forward(a, 0).start()
        for d in (1, 7, 2, 6, 3, 5, 4):
            in_arrival(a, d).wait_recv()
            forward(a, d).start()

    landed(4)
    seg_fw = pltpu.make_async_remote_copy(
        segb.at[c], segb.at[c], fw_send.at[1, 0], fw_recv.at[1, 0],
        device_id={"frames": other}, device_id_type=MESH)
    seg_fw.start()
    lane = lax.broadcasted_iota(jnp.int32, (ROWS, HEAD_DIM), 1).astype(F32)

    def segment_rows(core, i):
        row = segb[core, i][0:1, :]
        return jnp.transpose(jnp.broadcast_to(row, (HEAD_DIM, 2 * HEAD_DIM)))[:ROWS]

    def own_rows(i, _):
        seg = segment_rows(c, i)
        eb[krows(c, i), :] = jnp.where(seg == lane, 1.0, 0.0).astype(BF16)
        hiding = jnp.where(lane > seg, HIDDEN, 0.0).astype(BF16)
        for j in range(BLOCKS):
            ab[j, i] = hiding[j * PIECE : (j + 1) * PIECE]
        return 0

    lax.fori_loop(0, CHIPS, own_rows, 0)
    seg_fw.wait_send()
    pltpu.make_async_remote_copy(
        segb.at[1 - c], segb.at[1 - c], fw_send.at[1, 0], fw_recv.at[1, 0],
        device_id={"frames": other}, device_id_type=MESH).wait_recv()

    def other_rows(i, _):
        eb[krows(1 - c, i), :] = jnp.where(segment_rows(1 - c, i) == lane, 1.0, 0.0).astype(BF16)
        return 0

    lax.fori_loop(0, CHIPS, other_rows, 0)

    share(0)
    landed(1)
    for d in range(CHIPS):
        forwarded(0, d).wait_recv()
    for i in range(ALL // KC):
        kt[:, i * KC : (i + 1) * KC] = jnp.transpose(kb[i * KC : (i + 1) * KC, :].astype(F32)).astype(BF16)

    def flat(ref, i):
        return ref[i].reshape(RB, HEAD_DIM)

    def pieces(array):
        return array.reshape(CHIPS, PIECE, HEAD_DIM)

    def block(i):
        return pl.ds(pl.multiple_of(i * RB, RB), RB)

    def weights_step(i, _):
        qx = jnp.concatenate([flat(qb, i), flat(ab, i)], axis=1)
        most = jnp.full((8, RB), -jnp.inf, F32)
        for j in range(ALL // KC):
            at = slice(j * KC, (j + 1) * KC)
            kx = jnp.concatenate([kb[at, :], eb[at, :]], axis=1)
            s = dot_rows(kx, qx)
            sb[at, :] = s
            most = jnp.maximum(most, jnp.max(s.reshape(KC // 8, 8, RB), axis=0))
        top = jnp.max(most, axis=0, keepdims=True) * SCALE2
        for j in range(ALL // KC):
            at = slice(j * KC, (j + 1) * KC)
            pb[i, at, :] = jnp.exp2(sb[at, :] * SCALE2 - top).astype(BF16)
        return 0

    lax.fori_loop(0, OWN // RB, weights_step, 0)

    share(2)
    for d in range(CHIPS):
        forwarded(2, d).wait_recv()
    vt[HEAD_DIM:, :] = jnp.ones((HEAD_DIM, ALL), BF16)
    for i in range(ALL // KC):
        vt[:HEAD_DIM, i * KC : (i + 1) * KC] = jnp.transpose(vb[i * KC : (i + 1) * KC, :].astype(F32)).astype(BF16)

    def output_step(i, _):
        both = jnp.transpose(dot_plain(vt[...], pb[i]))
        part = 1.0 / both[:, HEAD_DIM:]
        inv[block(i), :] = part
        obuf[i] = pieces((both[:, :HEAD_DIM] * part).astype(BF16))
        return 0

    lax.fori_loop(0, OWN // RB, output_step, 0)

    def back(a, to, source):
        if a == 0:
            return obuf.at[:, to], o_out.at[:, :, cols(source)]
        if a < 3:
            buf, out = ((dvb, dv_out), (dkb, dk_out))[a - 1]
            return buf.at[rows(to)], out.at[:, cols(source)]
        low, high = GROUPS[a - 3]
        span = pl.ds(low, high - low)
        return dqb.at[span, to], dq_out.at[span, :, cols(source)]

    def out_copy(a, d):
        src, dst = back(a, peer(d), z)
        return pltpu.make_async_remote_copy(
            src, dst, out_send.at[a, d], out_recv.at[a, d],
            device_id={"frames": peer(d) * 2 + c}, device_id_type=MESH)

    def out_arrival(a, d):
        source = lax.rem(z + CHIPS - d, CHIPS)
        src, dst = back(a, source, source)
        return pltpu.make_async_remote_copy(
            src, dst, out_send.at[a, d], out_recv.at[a, d],
            device_id={"frames": peer(d) * 2 + c}, device_id_type=MESH)

    def out_own(a):
        src, dst = back(a, z, z)
        return pltpu.make_async_copy(src, dst, out_loc.at[a])

    def send_back(a):
        for d in turns:
            out_copy(a, d).start()
        out_own(a).start()

    send_back(0)

    narrow = lax.broadcasted_iota(jnp.int32, (RB, HEAD_DIM), 1)
    ones = jnp.ones((KC, HEAD_DIM), BF16)

    def grad_step(i, _):
        low = flat(gb, i)
        g = low.astype(F32)
        part = inv[block(i), :]
        gn[block(i), :] = (g * part).astype(BF16)
        qn[block(i), :] = (flat(qb, i).astype(F32) * (part * SCALE)).astype(BF16)
        delta = -jnp.sum(g * flat(obuf, i).astype(F32), axis=1, keepdims=True)
        first = delta.astype(BF16).astype(F32)
        second = (delta - first).astype(BF16).astype(F32)
        third = delta - first - second
        cells = jnp.where(narrow == 0, first, jnp.where(narrow == 1, second, jnp.where(narrow == 2, third, 0.0)))
        gx = jnp.concatenate([low, cells.astype(BF16)], axis=1)
        for j in range(ALL // KC):
            at = slice(j * KC, (j + 1) * KC)
            vx = jnp.concatenate([vb[at, :], ones], axis=1)
            ds[i, at, :] = (pb[i, at, :].astype(F32) * dot_rows(vx, gx)).astype(BF16)
        dq = jnp.transpose(dot_plain(kt[...], ds[i]))
        dqb[i] = pieces((dq * (part * SCALE)).astype(BF16))
        return 0

    for group, (low, high) in enumerate(GROUPS):
        g_own(group).wait()
        for d in range(1, CHIPS):
            g_copy(group, d, z, lax.rem(z + CHIPS - d, CHIPS)).wait_recv()
        lax.fori_loop(low, high, grad_step, 0)
        send_back(3 + group)

    def terms(left, right, core, j):
        at = pl.ds(pl.multiple_of(core * OWN + j * RB, RB), RB)
        total = dot_plain(left[0, at, :], right[0:RB, :])
        for i in range(1, BLOCKS):
            total = total + dot_plain(left[i, at, :], right[i * RB : (i + 1) * RB, :])
        return total

    def swap(a, j):
        at = slice(j * RB, (j + 1) * RB)
        return pltpu.make_async_remote_copy(
            give.at[a, at], got.at[a, at], x_send.at[a, j], x_recv.at[a, j],
            device_id={"frames": other}, device_id_type=MESH)

    sums = ((pb, gn, dvb), (ds, qn, dkb))
    for a, (left, right, _) in enumerate(sums):
        for j in range(BLOCKS):
            give[a, j * RB : (j + 1) * RB, :] = terms(left, right, 1 - c, j)
            swap(a, j).start()
    for a, (left, right, result) in enumerate(sums):
        for j in range(BLOCKS):
            mine = terms(left, right, c, j)
            swap(a, j).wait()
            at = slice(j * RB, (j + 1) * RB)
            result[at, :] = (mine + got[a, at, :]).astype(BF16)
        send_back(1 + a)

    for d in range(1, CHIPS):
        for a in (4, 0, 1, 2):
            in_copy(a, d).wait_send()
        for group in range(len(GROUPS)):
            g_copy(group, d, peer(d), z).wait_send()
    for a in (0, 2):
        for d in range(CHIPS):
            forward(a, d).wait_send()
    for a in range(3 + len(GROUPS)):
        out_own(a).wait()
        for d in range(1, CHIPS):
            out_copy(a, d).wait_send()
            out_arrival(a, d).wait_recv()


def shards(queries, key_vectors, values, grad_output, segment_index):
    vmem, sems = pltpu.VMEM, pltpu.SemaphoreType.DMA
    any_spec = pl.BlockSpec(memory_space=pl.ANY)
    whole = jax.ShapeDtypeStruct(queries.shape, BF16)
    cut = jax.ShapeDtypeStruct((BLOCKS, PIECE, queries.shape[1]), BF16)
    by_block = (BLOCKS, CHIPS, PIECE, HEAD_DIM)
    found = pl.pallas_call(
        kernel,
        out_shape=[vmem(array.shape, BF16) for array in (cut, cut, whole, whole)],
        in_specs=[any_spec] * 5,
        out_specs=[any_spec] * 4,
        scratch_shapes=[
            vmem(by_block, BF16),
            vmem((ALL, HEAD_DIM), BF16),
            vmem((ALL, HEAD_DIM), BF16),
            vmem(by_block, BF16),
            vmem((1, ROWS), jnp.int32),
            vmem((8, 2 * HEAD_DIM), F32),
            vmem((2, CHIPS, 8, 2 * HEAD_DIM), F32),
            vmem((ALL, HEAD_DIM), BF16),
            vmem(by_block, BF16),
            vmem((2 * HEAD_DIM, ALL), BF16),
            vmem((HEAD_DIM, ALL), BF16),
            vmem((ALL, RB), F32),
            vmem((BLOCKS, ALL, RB), BF16),
            vmem((BLOCKS, ALL, RB), BF16),
            vmem((OWN, HEAD_DIM), F32),
            vmem(by_block, BF16),
            vmem((OWN, HEAD_DIM), BF16),
            vmem((OWN, HEAD_DIM), BF16),
            vmem((2, OWN, HEAD_DIM), F32),
            vmem((2, OWN, HEAD_DIM), F32),
            vmem(by_block, BF16),
            vmem((OWN, HEAD_DIM), BF16),
            vmem((OWN, HEAD_DIM), BF16),
            pltpu.SemaphoreType.DMA,
            sems((5, CHIPS)),
            sems((5, CHIPS)),
            sems((5,)),
            sems((len(GROUPS), CHIPS)),
            sems((len(GROUPS), CHIPS)),
            sems((len(GROUPS),)),
            sems((3, CHIPS)),
            sems((3, CHIPS)),
            sems((3 + len(GROUPS), CHIPS)),
            sems((3 + len(GROUPS), CHIPS)),
            sems((3 + len(GROUPS),)),
            sems((2, BLOCKS)),
            sems((2, BLOCKS)),
        ],
        compiler_params=pltpu.CompilerParams(
            collective_id=0, has_side_effects=True, vmem_limit_bytes=40 << 20
        ),
        cost_estimate=pl.CostEstimate(
            flops=12 * OWN * ALL * HEAD_DIM, bytes_accessed=8 * ROWS * 1024 * 2, transcendentals=OWN * ALL
        ),
    )(*[
        pltpu.with_memory_space_constraint(array, pltpu.HBM)
        for array in (
            queries.reshape(cut.shape), key_vectors, values, grad_output.reshape(cut.shape),
            segment_index.reshape(1, ROWS),
        )
    ])
    return pl.pallas_call(
        hand_over,
        out_shape=[whole] * 4,
        in_specs=[any_spec] * 4,
        out_specs=[any_spec] * 4,
        scratch_shapes=[sems((4,))],
    )(*[pltpu.with_memory_space_constraint(array.reshape(whole.shape), pltpu.VMEM) for array in found])


def hand_over(*refs):
    sources, outs, sem = refs[:4], refs[4:8], refs[8]
    copies = [pltpu.make_async_copy(src, out, sem.at[a]) for a, (src, out) in enumerate(zip(sources, outs))]
    for copy in copies:
        copy.start()
    for copy in copies:
        copy.wait()


def solution(mesh):
    wide = P(("dp", "frames"), "heads")
    return jax.shard_map(
        shards,
        mesh=mesh,
        in_specs=(wide, wide, wide, wide, P(("dp", "frames"))),
        out_specs=(wide, wide, wide, wide),
        check_vma=False,
    )
```

```python
import functools
import math

import jax
import jax.numpy as jnp
from jax import lax
from jax.experimental import pallas as pl
from jax.experimental.pallas import tpu as pltpu
from jax.sharding import PartitionSpec as P

HEAD_DIM = 128
MESH = pl.DeviceIdType.MESH
ROWS = 160
CHIPS = 8
OWN = CHIPS * ROWS
ALL = 2 * OWN
RB = 256
KC = 512
HIDDEN = -float(2**30)
SCALE = 1.0 / math.sqrt(HEAD_DIM)
SCALE2 = SCALE * math.log2(math.e)
PIECE = RB // CHIPS
BLOCKS = OWN // RB
GROUPS = ((0, 0, 2), (0, 2, 5), (1, 0, 3), (1, 3, 5))
ORDER = ((4, 4), (3, 5), (5, 3), (2, 6), (6, 2), (1, 7), (7, 1))
FAR_FIRST = (4, 3, 5, 2, 6, 1, 7)
F32, BF16 = jnp.float32, jnp.bfloat16


def dot_rows(a, b):
    return lax.dot_general(a, b, (((1,), (1,)), ((), ())), preferred_element_type=F32)


def dot_plain(a, b):
    return lax.dot_general(a, b, (((1,), (0,)), ((), ())), preferred_element_type=F32)


def kernel(
    q_ref, k_ref, v_ref, g_ref, seg_ref,
    oq_out, kv_out,
    kv_in, qg_in, kvb, qgb, segin, segown, segb, eb, ab, vt, kt, sb, pb, ds, inv, gn, qn,
    give, got, oqb, kvg,
    seg_sem, stage, in_send, in_recv, loc, fw_send, fw_recv, out_send, out_recv, out_loc, x_send, x_recv,
):
    me = lax.axis_index("frames")
    z, c = me // 2, lax.rem(me, 2)
    other = {"frames": z * 2 + 1 - c}

    def peer(d):
        return lax.rem(z + d, CHIPS)

    def chip(i):
        return {"frames": i * 2 + c}

    def cols(i):
        return pl.ds(pl.multiple_of(i * HEAD_DIM, HEAD_DIM), HEAD_DIM)

    def rows(i):
        return pl.ds(pl.multiple_of(i * ROWS, ROWS), ROWS)

    def krows(core, i):
        return pl.ds(pl.multiple_of((core * CHIPS + i) * ROWS, ROWS), ROWS)

    seg_copy = pltpu.make_async_copy(seg_ref, segin, seg_sem)
    seg_copy.start()
    stages = [
        pltpu.make_async_copy(src, dst, stage.at[a])
        for a, (src, dst) in enumerate(
            ((k_ref, kv_in.at[0]), (v_ref, kv_in.at[1]), (q_ref, qg_in.at[0]), (g_ref, qg_in.at[1]))
        )
    ]
    for copy in stages:
        copy.start()

    barrier = pltpu.get_barrier_semaphore()
    for d in FAR_FIRST:
        pl.semaphore_signal(barrier, inc=1, device_id=chip(peer(d)), device_id_type=MESH)
    pl.semaphore_signal(barrier, inc=1, device_id=other, device_id_type=MESH)
    seg_copy.wait()
    segown[:, :ROWS] = jnp.broadcast_to(segin[...].astype(F32), (8, ROWS))
    segown[:, ROWS:] = jnp.zeros((8, 2 * HEAD_DIM - ROWS), F32)
    for copy in stages:
        copy.wait()
    pl.semaphore_wait(barrier, CHIPS)

    def parts(a, head, source):
        if a == 0:
            return segown, segb.at[c, source]
        if a == 1:
            return kv_in.at[:, :, cols(head)], kvb.at[:, krows(c, source)]
        kind, low, high = GROUPS[a - 2]
        span = pl.ds(low, high - low)
        return qg_in.at[kind, span, :, cols(head)], qgb.at[kind, span, source]

    def in_copy(a, d):
        src, dst = parts(a, peer(d), z)
        return pltpu.make_async_remote_copy(
            src, dst, in_send.at[a, d], in_recv.at[a, d], device_id=chip(peer(d)), device_id_type=MESH)

    def in_arrival(a, d):
        src, dst = parts(a, z, lax.rem(z + CHIPS - d, CHIPS))
        return pltpu.make_async_remote_copy(
            src, dst, in_send.at[a, d], in_recv.at[a, d], device_id=chip(peer(d)), device_id_type=MESH)

    def own_copy(a):
        src, dst = parts(a, z, z)
        return pltpu.make_async_copy(src, dst, loc.at[a])

    turns = [a if a == b else jnp.where(c == 0, a, b) for a, b in ORDER]
    for a in range(2 + len(GROUPS)):
        for d in turns:
            in_copy(a, d).start()
        own_copy(a).start()

    def landed(a):
        own_copy(a).wait()
        for d in range(1, CHIPS):
            in_arrival(a, d).wait_recv()

    def forward(core, d):
        where = krows(core, lax.rem(z + CHIPS - d, CHIPS))
        return pltpu.make_async_remote_copy(
            kvb.at[:, where], kvb.at[:, where], fw_send.at[d], fw_recv.at[d], device_id=other, device_id_type=MESH)

    def seg_forward(core):
        return pltpu.make_async_remote_copy(
            segb.at[core], segb.at[core], fw_send.at[CHIPS], fw_recv.at[CHIPS], device_id=other, device_id_type=MESH)

    landed(0)
    seg_forward(c).start()
    lane = lax.broadcasted_iota(jnp.int32, (ROWS, HEAD_DIM), 1).astype(F32)

    def segment_rows(core, i):
        row = segb[core, i][0:1, :]
        return jnp.transpose(jnp.broadcast_to(row, (HEAD_DIM, 2 * HEAD_DIM)))[:ROWS]

    def own_rows(i, _):
        seg = segment_rows(c, i)
        eb[krows(c, i), :] = jnp.where(seg == lane, 1.0, 0.0).astype(BF16)
        hiding = jnp.where(lane > seg, HIDDEN, 0.0).astype(BF16)
        for j in range(BLOCKS):
            ab[j, i] = hiding[j * PIECE : (j + 1) * PIECE]
        return 0

    lax.fori_loop(0, CHIPS, own_rows, 0)
    seg_forward(c).wait_send()
    seg_forward(1 - c).wait_recv()

    def other_rows(i, _):
        eb[krows(1 - c, i), :] = jnp.where(segment_rows(1 - c, i) == lane, 1.0, 0.0).astype(BF16)
        return 0

    lax.fori_loop(0, CHIPS, other_rows, 0)
    vt[HEAD_DIM:, :] = jnp.ones((HEAD_DIM, ALL), BF16)

    own_copy(1).wait()
    forward(c, 0).start()
    for d in (1, 7, 2, 6, 3, 5, 4):
        in_arrival(1, d).wait_recv()
        forward(c, d).start()
    for d in range(CHIPS):
        forward(1 - c, d).wait_recv()
    for i in range(ALL // KC):
        at = slice(i * KC, (i + 1) * KC)
        vt[:HEAD_DIM, at] = jnp.transpose(kvb[1, at, :].astype(F32)).astype(BF16)
        kt[:, at] = jnp.transpose(kvb[0, at, :].astype(F32)).astype(BF16)

    def flat(ref, *i):
        return ref[i].reshape(RB, HEAD_DIM)

    def pieces(array):
        return array.reshape(CHIPS, PIECE, HEAD_DIM)

    def block(i):
        return pl.ds(pl.multiple_of(i * RB, RB), RB)

    def back(a, to, source):
        if a < 2:
            return kvg.at[a, rows(to)], kv_out.at[a, :, cols(source)]
        kind, low, high = GROUPS[a - 2]
        span = pl.ds(low, high - low)
        return oqb.at[kind, span, to], oq_out.at[kind, span, :, cols(source)]

    def out_copy(a, d):
        src, dst = back(a, peer(d), z)
        return pltpu.make_async_remote_copy(
            src, dst, out_send.at[a, d], out_recv.at[a, d], device_id=chip(peer(d)), device_id_type=MESH)

    def out_arrival(a, d):
        source = lax.rem(z + CHIPS - d, CHIPS)
        src, dst = back(a, source, source)
        return pltpu.make_async_remote_copy(
            src, dst, out_send.at[a, d], out_recv.at[a, d], device_id=chip(peer(d)), device_id_type=MESH)

    def out_own(a):
        src, dst = back(a, z, z)
        return pltpu.make_async_copy(src, dst, out_loc.at[a])

    def send_back(a):
        if a < 2:
            for to in range(CHIPS):

                @pl.when(to != z)
                def _():
                    out_copy(a, lax.rem(to - z + CHIPS, CHIPS)).start()

        else:
            for d in turns:
                out_copy(a, d).start()
        out_own(a).start()

    narrow = lax.broadcasted_iota(jnp.int32, (RB, HEAD_DIM), 1)
    ones = jnp.ones((KC, HEAD_DIM), BF16)

    def output_step(i, _):
        q = flat(qgb, 0, i)
        qx = jnp.concatenate([q, flat(ab, i)], axis=1)
        most = jnp.full((8, RB), -jnp.inf, F32)
        for j in range(ALL // KC):
            at = slice(j * KC, (j + 1) * KC)
            kx = jnp.concatenate([kvb[0, at, :], eb[at, :]], axis=1)
            s = dot_rows(kx, qx)
            sb[at, :] = s
            most = jnp.maximum(most, jnp.max(s.reshape(KC // 8, 8, RB), axis=0))
        top = jnp.max(most, axis=0, keepdims=True) * SCALE2
        for j in range(ALL // KC):
            at = slice(j * KC, (j + 1) * KC)
            pb[i, at, :] = jnp.exp2(sb[at, :] * SCALE2 - top).astype(BF16)
        both = jnp.transpose(dot_plain(vt[...], pb[i]))
        part = 1.0 / both[:, HEAD_DIM:]
        inv[block(i), :] = part
        oqb[0, i] = pieces((both[:, :HEAD_DIM] * part).astype(BF16))
        return 0

    def grad_step(i, _):
        low = flat(qgb, 1, i)
        part = inv[block(i), :]
        g = low.astype(F32)
        gn[block(i), :] = (g * part).astype(BF16)
        qn[block(i), :] = (flat(qgb, 0, i).astype(F32) * (part * SCALE)).astype(BF16)
        delta = -jnp.sum(g * flat(oqb, 0, i).astype(F32), axis=1, keepdims=True)
        first = delta.astype(BF16).astype(F32)
        second = (delta - first).astype(BF16).astype(F32)
        third = delta - first - second
        cells = jnp.where(narrow == 0, first, jnp.where(narrow == 1, second, jnp.where(narrow == 2, third, 0.0)))
        gx = jnp.concatenate([low, cells.astype(BF16)], axis=1)
        for j in range(ALL // KC):
            at = slice(j * KC, (j + 1) * KC)
            vx = jnp.concatenate([kvb[1, at, :], ones], axis=1)
            ds[i, at, :] = (pb[i, at, :].astype(F32) * dot_rows(vx, gx)).astype(BF16)
        dq = jnp.transpose(dot_plain(kt[...], ds[i]))
        oqb[1, i] = pieces((dq * (part * SCALE)).astype(BF16))
        return 0

    for group, (kind, low, high) in enumerate(GROUPS):
        landed(2 + group)
        lax.fori_loop(low, high, grad_step if kind else output_step, 0)
        send_back(2 + group)

    def terms(left, right, core, j):
        at = pl.ds(pl.multiple_of(core * OWN + j * RB, RB), RB)
        total = dot_plain(left[0, at, :], right[0:RB, :])
        for i in range(1, BLOCKS):
            total = total + dot_plain(left[i, at, :], right[i * RB : (i + 1) * RB, :])
        return total

    def swap(a, j):
        at = slice(j * RB, (j + 1) * RB)
        return pltpu.make_async_remote_copy(
            give.at[a, at], got.at[a, at], x_send.at[a, j], x_recv.at[a, j], device_id=other, device_id_type=MESH)

    sums = ((pb, gn), (ds, qn))
    for a, (left, right) in enumerate(sums):
        for j in range(BLOCKS):
            give[a, j * RB : (j + 1) * RB, :] = terms(left, right, 1 - c, j)
            swap(a, j).start()
    for a, (left, right) in enumerate(sums):
        for j in range(BLOCKS):
            mine = terms(left, right, c, j)
            swap(a, j).wait()
            at = slice(j * RB, (j + 1) * RB)
            kvg[a, at, :] = (mine + got[a, at, :]).astype(BF16)
        send_back(a)

    for a in range(2 + len(GROUPS)):
        for d in range(1, CHIPS):
            in_copy(a, d).wait_send()
    for d in range(CHIPS):
        forward(c, d).wait_send()
    for a in range(2 + len(GROUPS)):
        out_own(a).wait()
        for d in range(1, CHIPS):
            out_copy(a, d).wait_send()
            out_arrival(a, d).wait_recv()


def shards(queries, key_vectors, values, grad_output, segment_index):
    vmem, sems = pltpu.VMEM, pltpu.SemaphoreType.DMA
    any_spec = pl.BlockSpec(memory_space=pl.ANY)
    whole = jax.ShapeDtypeStruct(queries.shape, BF16)
    cut = (BLOCKS, PIECE, queries.shape[1])
    kinds = 2 + len(GROUPS)
    oq, kv = pl.pallas_call(
        kernel,
        out_shape=[vmem((2,) + cut, BF16), vmem((2,) + queries.shape, BF16)],
        in_specs=[any_spec] * 5,
        out_specs=[any_spec] * 2,
        scratch_shapes=[
            vmem((2,) + queries.shape, BF16),
            vmem((2,) + cut, BF16),
            vmem((2, ALL, HEAD_DIM), BF16),
            vmem((2, BLOCKS, CHIPS, PIECE, HEAD_DIM), BF16),
            vmem((1, ROWS), jnp.int32),
            vmem((8, 2 * HEAD_DIM), F32),
            vmem((2, CHIPS, 8, 2 * HEAD_DIM), F32),
            vmem((ALL, HEAD_DIM), BF16),
            vmem((BLOCKS, CHIPS, PIECE, HEAD_DIM), BF16),
            vmem((2 * HEAD_DIM, ALL), BF16),
            vmem((HEAD_DIM, ALL), BF16),
            vmem((ALL, RB), F32),
            vmem((BLOCKS, ALL, RB), BF16),
            vmem((BLOCKS, ALL, RB), BF16),
            vmem((OWN, HEAD_DIM), F32),
            vmem((OWN, HEAD_DIM), BF16),
            vmem((OWN, HEAD_DIM), BF16),
            vmem((2, OWN, HEAD_DIM), F32),
            vmem((2, OWN, HEAD_DIM), F32),
            vmem((2, BLOCKS, CHIPS, PIECE, HEAD_DIM), BF16),
            vmem((2, OWN, HEAD_DIM), BF16),
            sems,
            sems((4,)),
            sems((kinds, CHIPS)),
            sems((kinds, CHIPS)),
            sems((kinds,)),
            sems((CHIPS + 1,)),
            sems((CHIPS + 1,)),
            sems((kinds, CHIPS)),
            sems((kinds, CHIPS)),
            sems((kinds,)),
            sems((2, BLOCKS)),
            sems((2, BLOCKS)),
        ],
        compiler_params=pltpu.CompilerParams(
            collective_id=0, has_side_effects=True, vmem_limit_bytes=44 << 20
        ),
        cost_estimate=pl.CostEstimate(
            flops=12 * OWN * ALL * HEAD_DIM, bytes_accessed=8 * ROWS * 1024 * 2, transcendentals=OWN * ALL
        ),
    )(*[
        pltpu.with_memory_space_constraint(array, pltpu.HBM)
        for array in (
            queries.reshape(cut), key_vectors, values, grad_output.reshape(cut), segment_index.reshape(1, ROWS)
        )
    ])
    return pl.pallas_call(
        hand_over,
        out_shape=[whole] * 4,
        in_specs=[any_spec] * 2,
        out_specs=[any_spec] * 4,
        scratch_shapes=[sems((4,))],
    )(*[pltpu.with_memory_space_constraint(a.reshape((2,) + queries.shape), pltpu.VMEM) for a in (oq, kv)])


def hand_over(oq_ref, kv_ref, o_out, dq_out, dk_out, dv_out, sem):
    pairs = ((oq_ref.at[0], o_out), (oq_ref.at[1], dq_out), (kv_ref.at[0], dv_out), (kv_ref.at[1], dk_out))
    copies = [pltpu.make_async_copy(src, out, sem.at[a]) for a, (src, out) in enumerate(pairs)]
    for copy in copies:
        copy.start()
    for copy in copies:
        copy.wait()


def solution(mesh):
    wide = P(("dp", "frames"), "heads")
    return jax.shard_map(
        shards,
        mesh=mesh,
        in_specs=(wide, wide, wide, wide, P(("dp", "frames"))),
        out_specs=(wide, wide, wide, wide),
        check_vma=False,
    )
```

```python
import functools
import math

import jax
import jax.numpy as jnp
from jax import lax
from jax.experimental import pallas as pl
from jax.experimental.pallas import tpu as pltpu
from jax.sharding import PartitionSpec as P

HEAD_DIM = 128
MESH = pl.DeviceIdType.MESH
ROWS = 160
CHIPS = 8
OWN = CHIPS * ROWS
ALL = 2 * OWN
RB = 256
KC = 512
HIDDEN = -float(2**30)
SCALE = 1.0 / math.sqrt(HEAD_DIM)
SCALE2 = SCALE * math.log2(math.e)
PIECE = RB // CHIPS
BLOCKS = OWN // RB
GROUPS = ((0, 0, 2), (0, 2, 5), (1, 0, 3), (1, 3, 5))
ORDER = ((4, 4), (3, 5), (5, 3), (2, 6), (6, 2), (1, 7), (7, 1))
FAR_FIRST = (4, 3, 5, 2, 6, 1, 7)
F32, BF16 = jnp.float32, jnp.bfloat16


def dot_rows(a, b):
    return lax.dot_general(a, b, (((1,), (1,)), ((), ())), preferred_element_type=F32)


def dot_plain(a, b):
    return lax.dot_general(a, b, (((1,), (0,)), ((), ())), preferred_element_type=F32)


def kernel(
    q_ref, k_ref, v_ref, g_ref, seg_ref,
    oq_out, kv_out,
    kv_in, qg_in, kvb, qgb, segin, segown, segb, eb, ab, vt, kt, sb, pb, ds, inv, gn, qn,
    give, got, oqb, kvg,
    seg_sem, stage, in_send, in_recv, loc, fw_send, fw_recv, out_send, out_recv, out_loc, x_send, x_recv,
):
    me = lax.axis_index("frames")
    z, c = me // 2, lax.rem(me, 2)
    other = {"frames": z * 2 + 1 - c}

    def peer(d):
        return lax.rem(z + d, CHIPS)

    def chip(i):
        return {"frames": i * 2 + c}

    def cols(i):
        return pl.ds(pl.multiple_of(i * HEAD_DIM, HEAD_DIM), HEAD_DIM)

    def rows(i):
        return pl.ds(pl.multiple_of(i * ROWS, ROWS), ROWS)

    def krows(core, i):
        return pl.ds(pl.multiple_of((core * CHIPS + i) * ROWS, ROWS), ROWS)

    seg_copy = pltpu.make_async_copy(seg_ref, segin, seg_sem)
    seg_copy.start()
    stages = [
        pltpu.make_async_copy(src, dst, stage.at[a])
        for a, (src, dst) in enumerate(
            ((k_ref, kv_in.at[0]), (v_ref, kv_in.at[1]), (q_ref, qg_in.at[0]), (g_ref, qg_in.at[1]))
        )
    ]
    for copy in stages:
        copy.start()

    barrier = pltpu.get_barrier_semaphore()
    for d in FAR_FIRST:
        pl.semaphore_signal(barrier, inc=1, device_id=chip(peer(d)), device_id_type=MESH)
    pl.semaphore_signal(barrier, inc=1, device_id=other, device_id_type=MESH)
    seg_copy.wait()
    segown[:, :ROWS] = jnp.broadcast_to(segin[...].astype(F32), (8, ROWS))
    segown[:, ROWS:] = jnp.zeros((8, 2 * HEAD_DIM - ROWS), F32)
    for copy in stages:
        copy.wait()
    pl.semaphore_wait(barrier, CHIPS)

    def parts(a, head, source):
        if a == 0:
            return segown, segb.at[c, source]
        if a == 1:
            return kv_in.at[:, :, cols(head)], kvb.at[:, krows(c, source)]
        kind, low, high = GROUPS[a - 2]
        span = pl.ds(low, high - low)
        return qg_in.at[kind, span, :, cols(head)], qgb.at[kind, span, source]

    def in_copy(a, d):
        src, dst = parts(a, peer(d), z)
        return pltpu.make_async_remote_copy(
            src, dst, in_send.at[a], in_recv.at[a], device_id=chip(peer(d)), device_id_type=MESH)

    def in_all(a):
        if a == 0:
            size = segb.at[c, pl.ds(0, CHIPS - 1)]
        elif a == 1:
            size = kvb.at[:, pl.ds(0, (CHIPS - 1) * ROWS)]
        else:
            kind, low, high = GROUPS[a - 2]
            size = qgb.at[kind, pl.ds(low, high - low), pl.ds(0, CHIPS - 1)]
        return pltpu.make_async_remote_copy(
            size, size, in_send.at[a], in_recv.at[a], device_id=other, device_id_type=MESH)

    def own_copy(a):
        src, dst = parts(a, z, z)
        return pltpu.make_async_copy(src, dst, loc.at[a])

    turns = [a if a == b else jnp.where(c == 0, a, b) for a, b in ORDER]
    for a in range(2 + len(GROUPS)):
        for d in turns:
            in_copy(a, d).start()
        own_copy(a).start()

    def landed(a):
        own_copy(a).wait()
        in_all(a).wait_recv()

    def forward(core):
        where = pl.ds(pl.multiple_of(core * OWN, OWN), OWN)
        return pltpu.make_async_remote_copy(
            kvb.at[:, where], kvb.at[:, where], fw_send.at[0], fw_recv.at[0], device_id=other, device_id_type=MESH)

    def seg_forward(core):
        return pltpu.make_async_remote_copy(
            segb.at[core], segb.at[core], fw_send.at[1], fw_recv.at[1], device_id=other, device_id_type=MESH)

    landed(0)
    seg_forward(c).start()
    lane = lax.broadcasted_iota(jnp.int32, (ROWS, HEAD_DIM), 1).astype(F32)

    def segment_rows(core, i):
        row = segb[core, i][0:1, :]
        return jnp.transpose(jnp.broadcast_to(row, (HEAD_DIM, 2 * HEAD_DIM)))[:ROWS]

    def own_rows(i, _):
        seg = segment_rows(c, i)
        eb[krows(c, i), :] = jnp.where(seg == lane, 1.0, 0.0).astype(BF16)
        hiding = jnp.where(lane > seg, HIDDEN, 0.0).astype(BF16)
        for j in range(BLOCKS):
            ab[j, i] = hiding[j * PIECE : (j + 1) * PIECE]
        return 0

    lax.fori_loop(0, CHIPS, own_rows, 0)
    seg_forward(c).wait_send()
    seg_forward(1 - c).wait_recv()

    def other_rows(i, _):
        eb[krows(1 - c, i), :] = jnp.where(segment_rows(1 - c, i) == lane, 1.0, 0.0).astype(BF16)
        return 0

    lax.fori_loop(0, CHIPS, other_rows, 0)
    vt[HEAD_DIM:, :] = jnp.ones((HEAD_DIM, ALL), BF16)

    landed(1)
    forward(c).start()
    forward(1 - c).wait_recv()
    for i in range(ALL // KC):
        at = slice(i * KC, (i + 1) * KC)
        vt[:HEAD_DIM, at] = jnp.transpose(kvb[1, at, :].astype(F32)).astype(BF16)
        kt[:, at] = jnp.transpose(kvb[0, at, :].astype(F32)).astype(BF16)

    def flat(ref, *i):
        return ref[i].reshape(RB, HEAD_DIM)

    def pieces(array):
        return array.reshape(CHIPS, PIECE, HEAD_DIM)

    def block(i):
        return pl.ds(pl.multiple_of(i * RB, RB), RB)

    def back(a, to, source):
        if a < 2:
            return kvg.at[a, rows(to)], kv_out.at[a, :, cols(source)]
        kind, low, high = GROUPS[a - 2]
        span = pl.ds(low, high - low)
        return oqb.at[kind, span, to], oq_out.at[kind, span, :, cols(source)]

    def out_copy(a, d):
        src, dst = back(a, peer(d), z)
        return pltpu.make_async_remote_copy(
            src, dst, out_send.at[a], out_recv.at[a], device_id=chip(peer(d)), device_id_type=MESH)

    def out_all(a):
        seven = pl.ds(0, (CHIPS - 1) * HEAD_DIM)
        if a < 2:
            size = kv_out.at[a, :, seven]
        else:
            kind, low, high = GROUPS[a - 2]
            size = oq_out.at[kind, pl.ds(low, high - low), :, seven]
        return pltpu.make_async_remote_copy(
            size, size, out_send.at[a], out_recv.at[a], device_id=other, device_id_type=MESH)

    def out_own(a):
        src, dst = back(a, z, z)
        return pltpu.make_async_copy(src, dst, out_loc.at[a])

    def send_back(a):
        if a < 2:
            for to in range(CHIPS):

                @pl.when(to != z)
                def _():
                    out_copy(a, lax.rem(to - z + CHIPS, CHIPS)).start()

        else:
            for d in turns:
                out_copy(a, d).start()
        out_own(a).start()

    narrow = lax.broadcasted_iota(jnp.int32, (RB, HEAD_DIM), 1)
    ones = jnp.ones((KC, HEAD_DIM), BF16)

    def output_step(i, _):
        q = flat(qgb, 0, i)
        qx = jnp.concatenate([q, flat(ab, i)], axis=1)
        most = jnp.full((8, RB), -jnp.inf, F32)
        for j in range(ALL // KC):
            at = slice(j * KC, (j + 1) * KC)
            kx = jnp.concatenate([kvb[0, at, :], eb[at, :]], axis=1)
            s = dot_rows(kx, qx)
            sb[at, :] = s
            most = jnp.maximum(most, jnp.max(s.reshape(KC // 8, 8, RB), axis=0))
        top = jnp.max(most, axis=0, keepdims=True) * SCALE2
        for j in range(ALL // KC):
            at = slice(j * KC, (j + 1) * KC)
            pb[i, at, :] = jnp.exp2(sb[at, :] * SCALE2 - top).astype(BF16)
        both = jnp.transpose(dot_plain(vt[...], pb[i]))
        part = 1.0 / both[:, HEAD_DIM:]
        inv[block(i), :] = part
        oqb[0, i] = pieces((both[:, :HEAD_DIM] * part).astype(BF16))
        return 0

    def grad_step(i, _):
        low = flat(qgb, 1, i)
        part = inv[block(i), :]
        g = low.astype(F32)
        gn[block(i), :] = (g * part).astype(BF16)
        qn[block(i), :] = (flat(qgb, 0, i).astype(F32) * (part * SCALE)).astype(BF16)
        delta = -jnp.sum(g * flat(oqb, 0, i).astype(F32), axis=1, keepdims=True)
        first = delta.astype(BF16).astype(F32)
        second = (delta - first).astype(BF16).astype(F32)
        third = delta - first - second
        cells = jnp.where(narrow == 0, first, jnp.where(narrow == 1, second, jnp.where(narrow == 2, third, 0.0)))
        gx = jnp.concatenate([low, cells.astype(BF16)], axis=1)
        for j in range(ALL // KC):
            at = slice(j * KC, (j + 1) * KC)
            vx = jnp.concatenate([kvb[1, at, :], ones], axis=1)
            ds[i, at, :] = (pb[i, at, :].astype(F32) * dot_rows(vx, gx)).astype(BF16)
        dq = jnp.transpose(dot_plain(kt[...], ds[i]))
        oqb[1, i] = pieces((dq * (part * SCALE)).astype(BF16))
        return 0

    for group, (kind, low, high) in enumerate(GROUPS):
        landed(2 + group)
        lax.fori_loop(low, high, grad_step if kind else output_step, 0)
        send_back(2 + group)

    def terms(left, right, core, j):
        at = pl.ds(pl.multiple_of(core * OWN + j * RB, RB), RB)
        total = dot_plain(left[0, at, :], right[0:RB, :])
        for i in range(1, BLOCKS):
            total = total + dot_plain(left[i, at, :], right[i * RB : (i + 1) * RB, :])
        return total

    def swap(a, j):
        at = slice(j * RB, (j + 1) * RB)
        return pltpu.make_async_remote_copy(
            give.at[a, at], got.at[a, at], x_send.at[a], x_recv.at[a], device_id=other, device_id_type=MESH)

    sums = ((pb, gn), (ds, qn))
    for a, (left, right) in enumerate(sums):
        for j in range(BLOCKS):
            give[a, j * RB : (j + 1) * RB, :] = terms(left, right, 1 - c, j)
            swap(a, j).start()
    for a, (left, right) in enumerate(sums):
        for j in range(BLOCKS):
            sb[j * RB : (j + 1) * RB, :HEAD_DIM] = terms(left, right, c, j)
        pltpu.make_async_remote_copy(
            give.at[a], got.at[a], x_send.at[a], x_recv.at[a], device_id=other, device_id_type=MESH).wait()
        kvg[a] = (sb[:OWN, :HEAD_DIM] + got[a]).astype(BF16)
        send_back(a)

    for a in range(2 + len(GROUPS)):
        in_all(a).wait_send()
    forward(c).wait_send()
    for a in range(2 + len(GROUPS)):
        out_own(a).wait()
        out_all(a).wait()


def shards(queries, key_vectors, values, grad_output, segment_index):
    vmem, sems = pltpu.VMEM, pltpu.SemaphoreType.DMA
    any_spec = pl.BlockSpec(memory_space=pl.ANY)
    whole = jax.ShapeDtypeStruct(queries.shape, BF16)
    cut = (BLOCKS, PIECE, queries.shape[1])
    kinds = 2 + len(GROUPS)
    oq, kv = pl.pallas_call(
        kernel,
        out_shape=[vmem((2,) + cut, BF16), vmem((2,) + queries.shape, BF16)],
        in_specs=[any_spec] * 5,
        out_specs=[any_spec] * 2,
        scratch_shapes=[
            vmem((2,) + queries.shape, BF16),
            vmem((2,) + cut, BF16),
            vmem((2, ALL, HEAD_DIM), BF16),
            vmem((2, BLOCKS, CHIPS, PIECE, HEAD_DIM), BF16),
            vmem((1, ROWS), jnp.int32),
            vmem((8, 2 * HEAD_DIM), F32),
            vmem((2, CHIPS, 8, 2 * HEAD_DIM), F32),
            vmem((ALL, HEAD_DIM), BF16),
            vmem((BLOCKS, CHIPS, PIECE, HEAD_DIM), BF16),
            vmem((2 * HEAD_DIM, ALL), BF16),
            vmem((HEAD_DIM, ALL), BF16),
            vmem((ALL, RB), F32),
            vmem((BLOCKS, ALL, RB), BF16),
            vmem((BLOCKS, ALL, RB), BF16),
            vmem((OWN, HEAD_DIM), F32),
            vmem((OWN, HEAD_DIM), BF16),
            vmem((OWN, HEAD_DIM), BF16),
            vmem((2, OWN, HEAD_DIM), F32),
            vmem((2, OWN, HEAD_DIM), F32),
            vmem((2, BLOCKS, CHIPS, PIECE, HEAD_DIM), BF16),
            vmem((2, OWN, HEAD_DIM), BF16),
            sems,
            sems((4,)),
            sems((kinds,)),
            sems((kinds,)),
            sems((kinds,)),
            sems((2,)),
            sems((2,)),
            sems((kinds,)),
            sems((kinds,)),
            sems((kinds,)),
            sems((2,)),
            sems((2,)),
        ],
        compiler_params=pltpu.CompilerParams(
            collective_id=0, has_side_effects=True, vmem_limit_bytes=44 << 20
        ),
        cost_estimate=pl.CostEstimate(
            flops=12 * OWN * ALL * HEAD_DIM, bytes_accessed=8 * ROWS * 1024 * 2, transcendentals=OWN * ALL
        ),
    )(*[
        pltpu.with_memory_space_constraint(array, pltpu.HBM)
        for array in (
            queries.reshape(cut), key_vectors, values, grad_output.reshape(cut), segment_index.reshape(1, ROWS)
        )
    ])
    return pl.pallas_call(
        hand_over,
        out_shape=[whole] * 4,
        in_specs=[any_spec] * 2,
        out_specs=[any_spec] * 4,
        scratch_shapes=[sems((4,))],
    )(*[pltpu.with_memory_space_constraint(a.reshape((2,) + queries.shape), pltpu.VMEM) for a in (oq, kv)])


def hand_over(oq_ref, kv_ref, o_out, dq_out, dk_out, dv_out, sem):
    pairs = ((oq_ref.at[0], o_out), (oq_ref.at[1], dq_out), (kv_ref.at[0], dv_out), (kv_ref.at[1], dk_out))
    copies = [pltpu.make_async_copy(src, out, sem.at[a]) for a, (src, out) in enumerate(pairs)]
    for copy in copies:
        copy.start()
    for copy in copies:
        copy.wait()


def solution(mesh):
    wide = P(("dp", "frames"), "heads")
    return jax.shard_map(
        shards,
        mesh=mesh,
        in_specs=(wide, wide, wide, wide, P(("dp", "frames"))),
        out_specs=(wide, wide, wide, wide),
        check_vma=False,
    )
```

```python
import math

import jax
import jax.numpy as jnp
from jax import lax
from jax.experimental import pallas as pl
from jax.experimental.pallas import tpu as pltpu
from jax.sharding import PartitionSpec as P

HEAD_DIM = 128
MESH = pl.DeviceIdType.MESH
ROWS = 160
CHIPS = 8
OWN = CHIPS * ROWS
ALL = 2 * OWN
RB = 256
KC = 512
HIDDEN = -float(2**30)
SCALE = 1.0 / math.sqrt(HEAD_DIM)
SCALE2 = SCALE * math.log2(math.e)
PIECE = RB // CHIPS
BLOCKS = OWN // RB
GROUPS = ((0, 0, 3), (0, 3, 5), (1, 0, 2), (1, 2, 4), (1, 4, 5))
ORDER = ((4, 4), (3, 5), (5, 3), (2, 6), (6, 2), (1, 7), (7, 1))
FAR_FIRST = (4, 3, 5, 2, 6, 1, 7)
F32, BF16 = jnp.float32, jnp.bfloat16


def dot_rows(a, b):
    return lax.dot_general(a, b, (((1,), (1,)), ((), ())), preferred_element_type=F32)


def dot_plain(a, b):
    return lax.dot_general(a, b, (((1,), (0,)), ((), ())), preferred_element_type=F32)


def kernel(
    q_ref, k_ref, v_ref, g_ref, seg_ref,
    oq_out, kv_out,
    kv_in, qg_in, kvb, qgb, segin, segown, segb, eb, ab, vt, kt, sb, pb, ds, inv, gn, qn,
    give, got, oqb, kvg,
    seg_sem, stage, in_send, in_recv, loc, fw_send, fw_recv, out_send, out_recv, out_loc, x_send, x_recv,
):
    me = lax.axis_index("frames")
    z, c = me // 2, lax.rem(me, 2)
    other = {"frames": z * 2 + 1 - c}

    def peer(d):
        return lax.rem(z + d, CHIPS)

    def chip(i):
        return {"frames": i * 2 + c}

    def cols(i):
        return pl.ds(pl.multiple_of(i * HEAD_DIM, HEAD_DIM), HEAD_DIM)

    def rows(i):
        return pl.ds(pl.multiple_of(i * ROWS, ROWS), ROWS)

    def krows(core, i):
        return pl.ds(pl.multiple_of((core * CHIPS + i) * ROWS, ROWS), ROWS)

    barrier = pltpu.get_barrier_semaphore()
    for d in FAR_FIRST:
        pl.semaphore_signal(barrier, inc=1, device_id=chip(peer(d)), device_id_type=MESH)
    pl.semaphore_signal(barrier, inc=1, device_id=other, device_id_type=MESH)
    seg_copy = pltpu.make_async_copy(seg_ref, segin, seg_sem)
    seg_copy.start()
    stages = [
        pltpu.make_async_copy(src, dst, stage.at[a])
        for a, (src, dst) in enumerate(
            ((k_ref, kv_in.at[0]), (v_ref, kv_in.at[1]), (q_ref, qg_in.at[0]), (g_ref, qg_in.at[1]))
        )
    ]
    for copy in stages:
        copy.start()
    seg_copy.wait()
    segown[:, :ROWS] = jnp.broadcast_to(segin[...].astype(F32), (8, ROWS))
    segown[:, ROWS:] = jnp.zeros((8, 2 * HEAD_DIM - ROWS), F32)
    pl.semaphore_wait(barrier, CHIPS)

    def parts(a, head, source):
        if a == 0:
            return segown, segb.at[c, source]
        if a == 1:
            return kv_in.at[:, :, cols(head)], kvb.at[:, krows(c, source)]
        kind, low, high = GROUPS[a - 2]
        span = pl.ds(low, high - low)
        return qg_in.at[kind, span, :, cols(head)], qgb.at[kind, span, source]

    def in_copy(a, d):
        src, dst = parts(a, peer(d), z)
        return pltpu.make_async_remote_copy(
            src, dst, in_send.at[a], in_recv.at[a], device_id=chip(peer(d)), device_id_type=MESH)

    def in_all(a):
        if a == 0:
            size = segb.at[c, pl.ds(0, CHIPS - 1)]
        elif a == 1:
            size = kvb.at[:, pl.ds(0, (CHIPS - 1) * ROWS)]
        else:
            kind, low, high = GROUPS[a - 2]
            size = qgb.at[kind, pl.ds(low, high - low), pl.ds(0, CHIPS - 1)]
        return pltpu.make_async_remote_copy(
            size, size, in_send.at[a], in_recv.at[a], device_id=other, device_id_type=MESH)

    def own_copy(a):
        src, dst = parts(a, z, z)
        return pltpu.make_async_copy(src, dst, loc.at[a])

    turns = [a if a == b else jnp.where(c == 0, a, b) for a, b in ORDER]
    for a in range(2 + len(GROUPS)):
        if a in (1, 2):
            for copy in stages[2 * a - 2 : 2 * a]:
                copy.wait()
        for d in turns:
            in_copy(a, d).start()
        own_copy(a).start()

    def landed(a):
        own_copy(a).wait()
        in_all(a).wait_recv()

    def forward(core):
        where = pl.ds(pl.multiple_of(core * OWN, OWN), OWN)
        return pltpu.make_async_remote_copy(
            kvb.at[:, where], kvb.at[:, where], fw_send.at[0], fw_recv.at[0], device_id=other, device_id_type=MESH)

    def seg_forward(core):
        return pltpu.make_async_remote_copy(
            segb.at[core], segb.at[core], fw_send.at[1], fw_recv.at[1], device_id=other, device_id_type=MESH)

    landed(0)
    seg_forward(c).start()
    lane = lax.broadcasted_iota(jnp.int32, (ROWS, HEAD_DIM), 1).astype(F32)

    def segment_rows(core, i):
        row = segb[core, i][0:1, :]
        return jnp.transpose(jnp.broadcast_to(row, (HEAD_DIM, 2 * HEAD_DIM)))[:ROWS]

    def own_rows(i, _):
        seg = segment_rows(c, i)
        eb[krows(c, i), :] = jnp.where(seg == lane, 1.0, 0.0).astype(BF16)
        hiding = jnp.where(lane > seg, HIDDEN, 0.0).astype(BF16)
        for j in range(BLOCKS):
            ab[j, i] = hiding[j * PIECE : (j + 1) * PIECE]
        return 0

    lax.fori_loop(0, CHIPS, own_rows, 0)
    seg_forward(c).wait_send()
    seg_forward(1 - c).wait_recv()

    def other_rows(i, _):
        eb[krows(1 - c, i), :] = jnp.where(segment_rows(1 - c, i) == lane, 1.0, 0.0).astype(BF16)
        return 0

    lax.fori_loop(0, CHIPS, other_rows, 0)
    vt[HEAD_DIM:, :] = jnp.ones((HEAD_DIM, ALL), BF16)

    landed(1)
    forward(c).start()
    forward(1 - c).wait_recv()
    for i in range(ALL // KC):
        at = slice(i * KC, (i + 1) * KC)
        vt[:HEAD_DIM, at] = jnp.transpose(kvb[1, at, :].astype(F32)).astype(BF16)
        kt[:, at] = jnp.transpose(kvb[0, at, :].astype(F32)).astype(BF16)

    def flat(ref, *i):
        return ref[i].reshape(RB, HEAD_DIM)

    def pieces(array):
        return array.reshape(CHIPS, PIECE, HEAD_DIM)

    def block(i):
        return pl.ds(pl.multiple_of(i * RB, RB), RB)

    def back(a, to, source):
        if a < 2:
            return kvg.at[a, rows(to)], kv_out.at[a, :, cols(source)]
        kind, low, high = GROUPS[a - 2]
        span = pl.ds(low, high - low)
        return oqb.at[kind, span, to], oq_out.at[kind, span, :, cols(source)]

    def out_copy(a, d):
        src, dst = back(a, peer(d), z)
        return pltpu.make_async_remote_copy(
            src, dst, out_send.at[a], out_recv.at[a], device_id=chip(peer(d)), device_id_type=MESH)

    def out_all(a):
        seven = pl.ds(0, (CHIPS - 1) * HEAD_DIM)
        if a < 2:
            size = kv_out.at[a, :, seven]
        else:
            kind, low, high = GROUPS[a - 2]
            size = oq_out.at[kind, pl.ds(low, high - low), :, seven]
        return pltpu.make_async_remote_copy(
            size, size, out_send.at[a], out_recv.at[a], device_id=other, device_id_type=MESH)

    def out_own(a):
        src, dst = back(a, z, z)
        return pltpu.make_async_copy(src, dst, out_loc.at[a])

    def send_back(a):
        if a < 2:
            for to in range(CHIPS):

                @pl.when(to != z)
                def _():
                    out_copy(a, lax.rem(to - z + CHIPS, CHIPS)).start()

        else:
            for d in turns:
                out_copy(a, d).start()
        out_own(a).start()

    narrow = lax.broadcasted_iota(jnp.int32, (RB, HEAD_DIM), 1)
    ones = jnp.ones((KC, HEAD_DIM), BF16)

    def output_step(i, _):
        q = flat(qgb, 0, i)
        qx = jnp.concatenate([q, flat(ab, i)], axis=1)
        most = jnp.full((8, RB), -jnp.inf, F32)
        for j in range(ALL // KC):
            at = slice(j * KC, (j + 1) * KC)
            kx = jnp.concatenate([kvb[0, at, :], eb[at, :]], axis=1)
            s = dot_rows(kx, qx)
            sb[at, :] = s
            most = jnp.maximum(most, jnp.max(s.reshape(KC // 8, 8, RB), axis=0))
        top = jnp.max(most, axis=0, keepdims=True) * SCALE2
        for j in range(ALL // KC):
            at = slice(j * KC, (j + 1) * KC)
            pb[i, at, :] = jnp.exp2(sb[at, :] * SCALE2 - top).astype(BF16)
        both = jnp.transpose(dot_plain(vt[...], pb[i]))
        part = 1.0 / both[:, HEAD_DIM:]
        inv[block(i), :] = part
        oqb[0, i] = pieces((both[:, :HEAD_DIM] * part).astype(BF16))
        return 0

    def grad_step(i, _):
        low = flat(qgb, 1, i)
        part = inv[block(i), :]
        g = low.astype(F32)
        gn[block(i), :] = (g * part).astype(BF16)
        qn[block(i), :] = (flat(qgb, 0, i).astype(F32) * (part * SCALE)).astype(BF16)
        delta = -jnp.sum(g * flat(oqb, 0, i).astype(F32), axis=1, keepdims=True)
        first = delta.astype(BF16).astype(F32)
        second = (delta - first).astype(BF16).astype(F32)
        third = delta - first - second
        cells = jnp.where(narrow == 0, first, jnp.where(narrow == 1, second, jnp.where(narrow == 2, third, 0.0)))
        gx = jnp.concatenate([low, cells.astype(BF16)], axis=1)
        for j in range(ALL // KC):
            at = slice(j * KC, (j + 1) * KC)
            vx = jnp.concatenate([kvb[1, at, :], ones], axis=1)
            ds[i, at, :] = (pb[i, at, :].astype(F32) * dot_rows(vx, gx)).astype(BF16)
        dq = jnp.transpose(dot_plain(kt[...], ds[i]))
        oqb[1, i] = pieces((dq * (part * SCALE)).astype(BF16))
        return 0

    for group, (kind, low, high) in enumerate(GROUPS):
        landed(2 + group)
        lax.fori_loop(low, high, grad_step if kind else output_step, 0)
        send_back(2 + group)

    def terms(left, right, core, j):
        at = pl.ds(pl.multiple_of(core * OWN + j * RB, RB), RB)
        total = dot_plain(left[0, at, :], right[0:RB, :])
        for i in range(1, BLOCKS):
            total = total + dot_plain(left[i, at, :], right[i * RB : (i + 1) * RB, :])
        return total

    def swap(a, j):
        at = slice(j * RB, (j + 1) * RB)
        return pltpu.make_async_remote_copy(
            give.at[a, at], got.at[a, at], x_send.at[a], x_recv.at[a], device_id=other, device_id_type=MESH)

    sums = ((pb, gn), (ds, qn))
    for a, (left, right) in enumerate(sums):
        for j in range(BLOCKS):
            give[a, j * RB : (j + 1) * RB, :] = terms(left, right, 1 - c, j)
            swap(a, j).start()
    for a, (left, right) in enumerate(sums):
        for j in range(BLOCKS):
            sb[j * RB : (j + 1) * RB, :HEAD_DIM] = terms(left, right, c, j)
        pltpu.make_async_remote_copy(
            give.at[a], got.at[a], x_send.at[a], x_recv.at[a], device_id=other, device_id_type=MESH).wait()
        kvg[a] = (sb[:OWN, :HEAD_DIM] + got[a]).astype(BF16)
        send_back(a)

    for a in range(2 + len(GROUPS)):
        in_all(a).wait_send()
    forward(c).wait_send()
    for a in range(2 + len(GROUPS)):
        out_own(a).wait()
        out_all(a).wait()


def shards(queries, key_vectors, values, grad_output, segment_index):
    vmem, sems = pltpu.VMEM, pltpu.SemaphoreType.DMA
    any_spec = pl.BlockSpec(memory_space=pl.ANY)
    whole = jax.ShapeDtypeStruct(queries.shape, BF16)
    cut = (BLOCKS, PIECE, queries.shape[1])
    kinds = 2 + len(GROUPS)
    oq, kv = pl.pallas_call(
        kernel,
        out_shape=[vmem((2,) + cut, BF16), vmem((2,) + queries.shape, BF16)],
        in_specs=[any_spec] * 5,
        out_specs=[any_spec] * 2,
        scratch_shapes=[
            vmem((2,) + queries.shape, BF16),
            vmem((2,) + cut, BF16),
            vmem((2, ALL, HEAD_DIM), BF16),
            vmem((2, BLOCKS, CHIPS, PIECE, HEAD_DIM), BF16),
            vmem((1, ROWS), jnp.int32),
            vmem((8, 2 * HEAD_DIM), F32),
            vmem((2, CHIPS, 8, 2 * HEAD_DIM), F32),
            vmem((ALL, HEAD_DIM), BF16),
            vmem((BLOCKS, CHIPS, PIECE, HEAD_DIM), BF16),
            vmem((2 * HEAD_DIM, ALL), BF16),
            vmem((HEAD_DIM, ALL), BF16),
            vmem((ALL, RB), F32),
            vmem((BLOCKS, ALL, RB), BF16),
            vmem((BLOCKS, ALL, RB), BF16),
            vmem((OWN, HEAD_DIM), F32),
            vmem((OWN, HEAD_DIM), BF16),
            vmem((OWN, HEAD_DIM), BF16),
            vmem((2, OWN, HEAD_DIM), F32),
            vmem((2, OWN, HEAD_DIM), F32),
            vmem((2, BLOCKS, CHIPS, PIECE, HEAD_DIM), BF16),
            vmem((2, OWN, HEAD_DIM), BF16),
            sems,
            sems((4,)),
            sems((kinds,)),
            sems((kinds,)),
            sems((kinds,)),
            sems((2,)),
            sems((2,)),
            sems((kinds,)),
            sems((kinds,)),
            sems((kinds,)),
            sems((2,)),
            sems((2,)),
        ],
        compiler_params=pltpu.CompilerParams(
            collective_id=0, has_side_effects=True, vmem_limit_bytes=44 << 20
        ),
        cost_estimate=pl.CostEstimate(
            flops=12 * OWN * ALL * HEAD_DIM, bytes_accessed=8 * ROWS * 1024 * 2, transcendentals=OWN * ALL
        ),
    )(*[
        pltpu.with_memory_space_constraint(array, pltpu.HBM)
        for array in (
            queries.reshape(cut), key_vectors, values, grad_output.reshape(cut), segment_index.reshape(1, ROWS)
        )
    ])
    return pl.pallas_call(
        hand_over,
        out_shape=[whole] * 4,
        in_specs=[any_spec] * 2,
        out_specs=[any_spec] * 4,
        scratch_shapes=[sems((4,))],
    )(*[pltpu.with_memory_space_constraint(a.reshape((2,) + queries.shape), pltpu.VMEM) for a in (oq, kv)])


def hand_over(oq_ref, kv_ref, o_out, dq_out, dk_out, dv_out, sem):
    pairs = ((oq_ref.at[0], o_out), (oq_ref.at[1], dq_out), (kv_ref.at[0], dv_out), (kv_ref.at[1], dk_out))
    copies = [pltpu.make_async_copy(src, out, sem.at[a]) for a, (src, out) in enumerate(pairs)]
    for copy in copies:
        copy.start()
    for copy in copies:
        copy.wait()


def solution(mesh):
    wide = P(("dp", "frames"), "heads")
    return jax.shard_map(
        shards,
        mesh=mesh,
        in_specs=(wide, wide, wide, wide, P(("dp", "frames"))),
        out_specs=(wide, wide, wide, wide),
        check_vma=False,
    )
```

```python
import functools
import math

import jax
import jax.numpy as jnp
from jax import lax
from jax.experimental import pallas as pl
from jax.experimental.pallas import tpu as pltpu
from jax.sharding import PartitionSpec as P

HEAD_DIM = 128
MESH = pl.DeviceIdType.MESH
ROWS = 160
CHIPS = 8
OWN = CHIPS * ROWS
ALL = 2 * OWN
RB = 256
KC = 512
HIDDEN = -float(2**30)
SCALE = 1.0 / math.sqrt(HEAD_DIM)
SCALE2 = SCALE * math.log2(math.e)
PIECE = RB // CHIPS
BLOCKS = OWN // RB
GROUPS = ((0, 0, 2), (0, 2, 5), (1, 0, 3), (1, 3, 5))
ORDER = ((4, 4), (3, 5), (5, 3), (2, 6), (6, 2), (1, 7), (7, 1))
FAR_FIRST = (4, 3, 5, 2, 6, 1, 7)
F32, BF16 = jnp.float32, jnp.bfloat16


def dot_rows(a, b):
    return lax.dot_general(a, b, (((1,), (1,)), ((), ())), preferred_element_type=F32)


def dot_plain(a, b):
    return lax.dot_general(a, b, (((1,), (0,)), ((), ())), preferred_element_type=F32)


def kernel(
    q_ref, k_ref, v_ref, g_ref, seg_ref,
    oq_out, kv_out,
    kv_in, qg_in, kvb, qgb, segin, segown, segb, eb, ab, vt, kt, sb, pb, ds, inv, gn, qn,
    give, got, oqb, kvg,
    seg_sem, stage, in_send, in_recv, fw_send, fw_recv, out_send, out_recv, x_send, x_recv,
):
    me = lax.axis_index("frames")
    z, c = me // 2, lax.rem(me, 2)
    other = {"frames": z * 2 + 1 - c}

    def peer(d):
        return lax.rem(z + d, CHIPS)

    def chip(i):
        return {"frames": i * 2 + c}

    def cols(i):
        return pl.ds(pl.multiple_of(i * HEAD_DIM, HEAD_DIM), HEAD_DIM)

    def rows(i):
        return pl.ds(pl.multiple_of(i * ROWS, ROWS), ROWS)

    def krows(core, i):
        return pl.ds(pl.multiple_of((core * CHIPS + i) * ROWS, ROWS), ROWS)

    seg_copy = pltpu.make_async_copy(seg_ref, segin, seg_sem)
    seg_copy.start()
    stages = [
        pltpu.make_async_copy(src, dst, stage.at[a])
        for a, (src, dst) in enumerate(
            ((k_ref, kv_in.at[0]), (v_ref, kv_in.at[1]), (q_ref, qg_in.at[0]), (g_ref, qg_in.at[1]))
        )
    ]
    for copy in stages:
        copy.start()

    barrier = pltpu.get_barrier_semaphore()
    for d in FAR_FIRST:
        pl.semaphore_signal(barrier, inc=1, device_id=chip(peer(d)), device_id_type=MESH)
    pl.semaphore_signal(barrier, inc=1, device_id=other, device_id_type=MESH)
    seg_copy.wait()
    segown[:, :ROWS] = jnp.broadcast_to(segin[...].astype(F32), (8, ROWS))
    segown[:, ROWS:] = jnp.zeros((8, 2 * HEAD_DIM - ROWS), F32)
    for copy in stages:
        copy.wait()
    pl.semaphore_wait(barrier, CHIPS)

    def parts(a, head, source):
        if a == 0:
            return segown, segb.at[c, source]
        if a == 1:
            return kv_in.at[:, :, cols(head)], kvb.at[:, krows(c, source)]
        kind, low, high = GROUPS[a - 2]
        span = pl.ds(low, high - low)
        return qg_in.at[kind, span, :, cols(head)], qgb.at[kind, span, source]

    def in_copy(a, d):
        src, dst = parts(a, peer(d), z)
        return pltpu.make_async_remote_copy(
            src, dst, in_send, in_recv.at[a], device_id=chip(peer(d)), device_id_type=MESH)

    def in_all(a):
        if a == 0:
            size = segb.at[c]
        elif a == 1:
            size = kvb.at[:, pl.ds(0, OWN)]
        else:
            kind, low, high = GROUPS[a - 2]
            size = qgb.at[kind, pl.ds(low, high - low)]
        return pltpu.make_async_remote_copy(
            size, size, in_send, in_recv.at[a], device_id=other, device_id_type=MESH)

    def own_copy(a):
        src, dst = parts(a, z, z)
        return pltpu.make_async_copy(src, dst, in_recv.at[a])

    turns = [a if a == b else jnp.where(c == 0, a, b) for a, b in ORDER]
    for a in range(2 + len(GROUPS)):
        for d in turns:
            in_copy(a, d).start()
        own_copy(a).start()

    def landed(a):
        in_all(a).wait_recv()

    def forward(core):
        where = pl.ds(pl.multiple_of(core * OWN, OWN), OWN)
        return pltpu.make_async_remote_copy(
            kvb.at[:, where], kvb.at[:, where], fw_send.at[0], fw_recv.at[0], device_id=other, device_id_type=MESH)

    def seg_forward(core):
        return pltpu.make_async_remote_copy(
            segb.at[core], segb.at[core], fw_send.at[1], fw_recv.at[1], device_id=other, device_id_type=MESH)

    landed(0)
    seg_forward(c).start()
    lane = lax.broadcasted_iota(jnp.int32, (ROWS, HEAD_DIM), 1).astype(F32)

    def segment_rows(core, i):
        row = segb[core, i][0:1, :]
        return jnp.transpose(jnp.broadcast_to(row, (HEAD_DIM, 2 * HEAD_DIM)))[:ROWS]

    def own_rows(i, _):
        seg = segment_rows(c, i)
        eb[krows(c, i), :] = jnp.where(seg == lane, 1.0, 0.0).astype(BF16)
        hiding = jnp.where(lane > seg, HIDDEN, 0.0).astype(BF16)
        for j in range(BLOCKS):
            ab[j, i] = hiding[j * PIECE : (j + 1) * PIECE]
        return 0

    lax.fori_loop(0, CHIPS, own_rows, 0)
    seg_forward(c).wait_send()
    seg_forward(1 - c).wait_recv()

    def other_rows(i, _):
        eb[krows(1 - c, i), :] = jnp.where(segment_rows(1 - c, i) == lane, 1.0, 0.0).astype(BF16)
        return 0

    lax.fori_loop(0, CHIPS, other_rows, 0)
    vt[HEAD_DIM:, :] = jnp.ones((HEAD_DIM, ALL), BF16)

    landed(1)
    forward(c).start()
    forward(1 - c).wait_recv()
    for i in range(ALL // KC):
        at = slice(i * KC, (i + 1) * KC)
        vt[:HEAD_DIM, at] = jnp.transpose(kvb[1, at, :].astype(F32)).astype(BF16)
        kt[:, at] = jnp.transpose(kvb[0, at, :].astype(F32)).astype(BF16)

    def flat(ref, *i):
        return ref[i].reshape(RB, HEAD_DIM)

    def pieces(array):
        return array.reshape(CHIPS, PIECE, HEAD_DIM)

    def block(i):
        return pl.ds(pl.multiple_of(i * RB, RB), RB)

    def back(a, to, source):
        if a < 2:
            return kvg.at[a, rows(to)], kv_out.at[a, :, cols(source)]
        kind, low, high = GROUPS[a - 2]
        span = pl.ds(low, high - low)
        return oqb.at[kind, span, to], oq_out.at[kind, span, :, cols(source)]

    def out_copy(a, d):
        src, dst = back(a, peer(d), z)
        return pltpu.make_async_remote_copy(
            src, dst, out_send, out_recv.at[a], device_id=chip(peer(d)), device_id_type=MESH)

    def out_all(a):
        if a < 2:
            size = kv_out.at[a]
        else:
            kind, low, high = GROUPS[a - 2]
            size = oq_out.at[kind, pl.ds(low, high - low)]
        return pltpu.make_async_remote_copy(
            size, size, out_send, out_recv.at[a], device_id=other, device_id_type=MESH)

    def out_own(a):
        src, dst = back(a, z, z)
        return pltpu.make_async_copy(src, dst, out_recv.at[a])

    def send_back(a):
        if a < 2:
            for to in range(CHIPS):

                @pl.when(to != z)
                def _():
                    out_copy(a, lax.rem(to - z + CHIPS, CHIPS)).start()

        else:
            for d in turns:
                out_copy(a, d).start()
        out_own(a).start()

    narrow = lax.broadcasted_iota(jnp.int32, (RB, HEAD_DIM), 1)
    ones = jnp.ones((KC, HEAD_DIM), BF16)

    def output_step(i, _):
        q = flat(qgb, 0, i)
        qx = jnp.concatenate([q, flat(ab, i)], axis=1)
        most = jnp.full((8, RB), -jnp.inf, F32)
        for j in range(ALL // KC):
            at = slice(j * KC, (j + 1) * KC)
            kx = jnp.concatenate([kvb[0, at, :], eb[at, :]], axis=1)
            s = dot_rows(kx, qx)
            sb[at, :] = s
            most = jnp.maximum(most, jnp.max(s.reshape(KC // 8, 8, RB), axis=0))
        top = jnp.max(most, axis=0, keepdims=True) * SCALE2
        for j in range(ALL // KC):
            at = slice(j * KC, (j + 1) * KC)
            pb[i, at, :] = jnp.exp2(sb[at, :] * SCALE2 - top).astype(BF16)
        both = jnp.transpose(dot_plain(vt[...], pb[i]))
        part = 1.0 / both[:, HEAD_DIM:]
        inv[block(i), :] = part
        oqb[0, i] = pieces((both[:, :HEAD_DIM] * part).astype(BF16))
        return 0

    def grad_step(i, _):
        low = flat(qgb, 1, i)
        part = inv[block(i), :]
        g = low.astype(F32)
        gn[block(i), :] = (g * part).astype(BF16)
        qn[block(i), :] = (flat(qgb, 0, i).astype(F32) * (part * SCALE)).astype(BF16)
        delta = -jnp.sum(g * flat(oqb, 0, i).astype(F32), axis=1, keepdims=True)
        first = delta.astype(BF16).astype(F32)
        second = (delta - first).astype(BF16).astype(F32)
        third = delta - first - second
        cells = jnp.where(narrow == 0, first, jnp.where(narrow == 1, second, jnp.where(narrow == 2, third, 0.0)))
        gx = jnp.concatenate([low, cells.astype(BF16)], axis=1)
        for j in range(ALL // KC):
            at = slice(j * KC, (j + 1) * KC)
            vx = jnp.concatenate([kvb[1, at, :], ones], axis=1)
            ds[i, at, :] = (pb[i, at, :].astype(F32) * dot_rows(vx, gx)).astype(BF16)
        dq = jnp.transpose(dot_plain(kt[...], ds[i]))
        oqb[1, i] = pieces((dq * (part * SCALE)).astype(BF16))
        return 0

    for group, (kind, low, high) in enumerate(GROUPS):
        landed(2 + group)
        lax.fori_loop(low, high, grad_step if kind else output_step, 0)
        send_back(2 + group)

    def terms(left, right, core, j):
        at = pl.ds(pl.multiple_of(core * OWN + j * RB, RB), RB)
        total = dot_plain(left[0, at, :], right[0:RB, :])
        for i in range(1, BLOCKS):
            total = total + dot_plain(left[i, at, :], right[i * RB : (i + 1) * RB, :])
        return total

    def swap(a, j):
        at = slice(j * RB, (j + 1) * RB)
        return pltpu.make_async_remote_copy(
            give.at[a, at], got.at[a, at], x_send.at[a], x_recv.at[a], device_id=other, device_id_type=MESH)

    sums = ((pb, gn), (ds, qn))
    for a, (left, right) in enumerate(sums):
        for j in range(BLOCKS):
            give[a, j * RB : (j + 1) * RB, :] = terms(left, right, 1 - c, j)
            swap(a, j).start()
    for a, (left, right) in enumerate(sums):
        for j in range(BLOCKS):
            sb[j * RB : (j + 1) * RB, :HEAD_DIM] = terms(left, right, c, j)
        pltpu.make_async_remote_copy(
            give.at[a], got.at[a], x_send.at[a], x_recv.at[a], device_id=other, device_id_type=MESH).wait()
        kvg[a] = (sb[:OWN, :HEAD_DIM] + got[a]).astype(BF16)
        send_back(a)

    for a in range(2 + len(GROUPS)):
        out_all(a).wait_recv()
    forward(c).wait_send()
    for sem, sent in ((in_send, 7 * 172032), (out_send, 7 * 163840)):
        size = pb.at[0, pl.ds(0, sent // 512)]
        pltpu.make_async_remote_copy(
            size, size, sem, in_recv.at[0], device_id=other, device_id_type=MESH).wait_send()


def shards(queries, key_vectors, values, grad_output, segment_index):
    vmem, sems = pltpu.VMEM, pltpu.SemaphoreType.DMA
    any_spec = pl.BlockSpec(memory_space=pl.ANY)
    whole = jax.ShapeDtypeStruct(queries.shape, BF16)
    cut = (BLOCKS, PIECE, queries.shape[1])
    kinds = 2 + len(GROUPS)
    oq, kv = pl.pallas_call(
        kernel,
        out_shape=[vmem((2,) + cut, BF16), vmem((2,) + queries.shape, BF16)],
        in_specs=[any_spec] * 5,
        out_specs=[any_spec] * 2,
        scratch_shapes=[
            vmem((2,) + queries.shape, BF16),
            vmem((2,) + cut, BF16),
            vmem((2, ALL, HEAD_DIM), BF16),
            vmem((2, BLOCKS, CHIPS, PIECE, HEAD_DIM), BF16),
            vmem((1, ROWS), jnp.int32),
            vmem((8, 2 * HEAD_DIM), F32),
            vmem((2, CHIPS, 8, 2 * HEAD_DIM), F32),
            vmem((ALL, HEAD_DIM), BF16),
            vmem((BLOCKS, CHIPS, PIECE, HEAD_DIM), BF16),
            vmem((2 * HEAD_DIM, ALL), BF16),
            vmem((HEAD_DIM, ALL), BF16),
            vmem((ALL, RB), F32),
            vmem((BLOCKS, ALL, RB), BF16),
            vmem((BLOCKS, ALL, RB), BF16),
            vmem((OWN, HEAD_DIM), F32),
            vmem((OWN, HEAD_DIM), BF16),
            vmem((OWN, HEAD_DIM), BF16),
            vmem((2, OWN, HEAD_DIM), F32),
            vmem((2, OWN, HEAD_DIM), F32),
            vmem((2, BLOCKS, CHIPS, PIECE, HEAD_DIM), BF16),
            vmem((2, OWN, HEAD_DIM), BF16),
            sems,
            sems((4,)),
            sems,
            sems((kinds,)),
            sems((2,)),
            sems((2,)),
            sems,
            sems((kinds,)),
            sems((2,)),
            sems((2,)),
        ],
        compiler_params=pltpu.CompilerParams(
            collective_id=0, has_side_effects=True, vmem_limit_bytes=44 << 20
        ),
        cost_estimate=pl.CostEstimate(
            flops=12 * OWN * ALL * HEAD_DIM, bytes_accessed=8 * ROWS * 1024 * 2, transcendentals=OWN * ALL
        ),
    )(*[
        pltpu.with_memory_space_constraint(array, pltpu.HBM)
        for array in (
            queries.reshape(cut), key_vectors, values, grad_output.reshape(cut), segment_index.reshape(1, ROWS)
        )
    ])
    return pl.pallas_call(
        hand_over,
        out_shape=[whole] * 4,
        in_specs=[any_spec] * 2,
        out_specs=[any_spec] * 4,
        scratch_shapes=[sems((4,))],
    )(*[pltpu.with_memory_space_constraint(a.reshape((2,) + queries.shape), pltpu.VMEM) for a in (oq, kv)])


def hand_over(oq_ref, kv_ref, o_out, dq_out, dk_out, dv_out, sem):
    pairs = ((oq_ref.at[0], o_out), (oq_ref.at[1], dq_out), (kv_ref.at[0], dv_out), (kv_ref.at[1], dk_out))
    copies = [pltpu.make_async_copy(src, out, sem.at[a]) for a, (src, out) in enumerate(pairs)]
    for copy in copies:
        copy.start()
    for copy in copies:
        copy.wait()


def solution(mesh):
    wide = P(("dp", "frames"), "heads")
    return jax.shard_map(
        shards,
        mesh=mesh,
        in_specs=(wide, wide, wide, wide, P(("dp", "frames"))),
        out_specs=(wide, wide, wide, wide),
        check_vma=False,
    )
```
